256 devices in a mesh: chan: 8 (over z), rad: 32 (over y, x, core).
Axes of the slice: x: 4, y: 4, z: 8, core: 2. Of those that a mesh axis runs over, the one named last changes fastest.
Arguments:
- wavefunc: float32 [2, 2048, 16384], P(None, 'chan', 'rad'), may hold values from -6 to 6
- orbitals: float32 [9, 16384], P(None, 'rad'), may hold values from -6 to 6
- channel_orbital: int32 [2048], P('chan'), may hold values from 0 to 8
- channel_l: int32 [2048], P('chan'), may hold values from 0 to 400
- row_order: int32 [144], replicated, may hold values from 0 to 15
- density_coupling: float32 [144, 2048], P(None, 'chan'), may hold values from -0.125 to 0.125
- field_coupling: float32 [2048, 144], P('chan'), may hold values from -6 to 6
Outputs:
- advanced: float32 [2, 2048, 16384], P(None, 'chan', 'rad')
The draws below stay inside these ranges and needn't reach their ends.
All inputs are finite; a program needn't handle non-finite values.
Results may differ from the reference program's by a relative error of at most 0.00021.
Values sent between devices are 32-bit elements; how exact they have to be, the bound alone decides.
A program may use at most 64 MiB of HBM per device.

```python
import jax
import jax.numpy as jnp
from jax import lax

CH = 2048
ORB = 9
NK = 16
LMAX = 400
SWEEPS = 4
M = 144
NR = 16384


def with_ends(result, stream_key, smallest, largest):
    dims = result.shape
    place = [jax.random.randint(jax.random.fold_in(stream_key, axis), (), 0, dims[axis]) for axis in range(len(dims))]
    result = result.at[tuple(place)].set(smallest)
    longest = dims.index(max(dims))
    place[longest] = (place[longest] + 1) % dims[longest]
    return result.at[tuple(place)].set(largest)


def level_of(key, shape, split, low, top_value):
    factor_of, own = 1.0, jax.random.fold_in(key, 6)
    for axis_at, blocks in split:
        draws = jnp.exp(jax.random.uniform(jax.random.fold_in(own, axis_at), (blocks,), jnp.float32, low / len(split), top_value / len(split)))
        factor_of = factor_of * jnp.repeat(draws, shape[axis_at] // blocks).reshape([-1 if axis == axis_at else 1 for axis in range(len(shape))])
    return factor_of


def scatter_about(key, extent, spread, reach, shards=(), kind=jnp.bfloat16):
    result = jax.random.normal(key, extent, jnp.float32) * spread
    if len(shards) > 0:
        result = level_of(key, extent, shards, -0.22, 0.18) * result
    return jnp.clip(result, min=-reach, max=reach).astype(kind)


def setup_inputs(seed: int = 0) -> dict:
    key_of = jax.random.split(jax.random.key(seed), 8)
    wavefunc = scatter_about(key_of[0], (2, CH, NR), 1.0, 6.0, ((1, 8), (2, 32)), jnp.float32)
    orbitals = scatter_about(key_of[1], (ORB, NR), 1.0, 6.0, ((1, 32),), jnp.float32)
    channel_orbital = with_ends(jax.random.randint(key_of[2], (CH,), 0, ORB), jax.random.fold_in(key_of[2], 1), 0, ORB - 1).astype(jnp.int32)
    channel_l = with_ends(jax.random.randint(key_of[3], (CH,), 0, LMAX + 1), jax.random.fold_in(key_of[3], 1), 0, LMAX).astype(jnp.int32)
    row_order = with_ends(jax.random.randint(key_of[4], (M,), 0, NK), jax.random.fold_in(key_of[4], 1), 0, NK - 1).astype(jnp.int32)
    density_coupling = scatter_about(key_of[5], (M, CH), CH ** -0.5, 0.125, ((1, 8),), jnp.float32)
    field_coupling = scatter_about(key_of[6], (CH, M), (0.2 * (NR / M) ** 0.5), 6.0, ((0, 8),), jnp.float32)
    return dict(wavefunc=wavefunc, orbitals=orbitals, channel_orbital=channel_orbital, channel_l=channel_l, row_order=row_order, density_coupling=density_coupling, field_coupling=field_coupling)


def tables(count, orders):
    index = jnp.arange(count, dtype=jnp.float32)
    radius = 8.0 + 400.0 * (index + 0.5) / count
    scaled = radius / 408.0
    power_up = jnp.exp(orders.astype(jnp.float32)[:, None] * jnp.log(scaled)[None, :])
    power_down = 1.0 / (power_up * scaled[None, :])
    return radius, power_up, power_down


def reference(wavefunc, orbitals, channel_orbital, channel_l, row_order, density_coupling, field_coupling):
    count = wavefunc.shape[2]
    delta = (400.0 / 408.0) / count
    radius, power_up, power_down = tables(count, row_order)
    orbital_of = orbitals[channel_orbital]
    ell = channel_l.astype(jnp.float32)
    cent = (ell * (ell + 1.0))[:, None] / (4.0 * radius * radius)[None, :]
    diag = 0.5 + cent

    def operate(field_in):
        padded = jnp.pad(field_in, ((0, 0), (0, 0), (1, 1)))
        kinetic = 0.25 * (2.0 * field_in - padded[:, :, :-2] - padded[:, :, 2:])
        weighted = field_in * orbital_of[None]
        rho = jnp.einsum("mc,scr->smr", density_coupling, weighted, precision=lax.Precision.HIGHEST)
        inner = jnp.cumsum(rho * power_up[None] * delta, axis=2)
        outer_terms = rho * power_down[None] * delta
        outer_rev = jnp.flip(jnp.cumsum(jnp.flip(outer_terms, 2), axis=2), 2)
        outer_after = jnp.concatenate([outer_rev[:, :, 1:], jnp.zeros_like(outer_rev[:, :, :1])], axis=2)
        potential = power_down[None] * inner + power_up[None] * outer_after
        mixed = jnp.einsum("cm,smr->scr", field_coupling, potential, precision=lax.Precision.HIGHEST)
        return kinetic + cent[None] * field_in + mixed * orbital_of[None]

    applied = operate(wavefunc)
    rhs_re = wavefunc[0] + applied[1]
    rhs_im = wavefunc[1] - applied[0]
    current = wavefunc
    for sweep in range(SWEEPS):
        offdiag = operate(current) - diag[None] * current
        num_re = rhs_re + offdiag[1]
        num_im = rhs_im - offdiag[0]
        scale = 1.0 / (1.0 + diag * diag)
        current = jnp.stack([(num_re + diag * num_im) * scale, (num_im - diag * num_re) * scale])
    return current
```

```python
import functools

import jax
import jax.numpy as jnp
from jax import lax
from jax.experimental import pallas as pl
from jax.experimental.pallas import tpu as pltpu
from jax.sharding import PartitionSpec as P

SWEEPS = 4
MESH = pl.DeviceIdType.MESH
F32 = jnp.float32
BF16 = jnp.bfloat16
LANES = 128
SPAN = 400.0 / 408.0

RS_PLAN = ((-4, -2), (-3, -1), (3, 1), (-1, -1), (1, 1), (-2, -2), (2, 2))
AG_PLAN = ((0, 2), (0, -2), (0, 1), (0, -1), (-2, 2), (-2, 1), (2, -1))
ROWS_STEP = 32


def split2(x):
    hi = x.astype(BF16)
    return hi, (x - hi.astype(F32)).astype(BF16)


def dot(a, b):
    return jnp.dot(a, b, preferred_element_type=F32)


def as_column(row):
    eight = jnp.broadcast_to(row, (8, row.shape[1]))
    first = lax.broadcasted_iota(jnp.int32, (8, LANES), 0) == 0
    return lax.dot_general(
        eight,
        jnp.where(first, 1.0, 0.0).astype(F32),
        (((0,), (0,)), ((), ())),
        precision=lax.Precision.HIGHEST,
        preferred_element_type=F32,
    )


def kernel(
    sizes,
    wave_hbm,
    orbitals_ref,
    which_ref,
    ell_ref,
    order_ref,
    density_ref,
    coupling_ref,
    out_hbm,
    vbuf,
    rhs,
    orb,
    diag,
    scl,
    field,
    up_t,
    dn_t,
    d_hi,
    d_lo,
    f_hi,
    f_lo,
    rho,
    pot,
    rsbuf,
    ca_src,
    ca_buf,
    cb_src,
    cb_buf,
    cc_src,
    cc_buf,
    io_sem,
    rs_s,
    rs_r,
    ag_s,
    ag_r,
    ca_s,
    ca_r,
    cb_s,
    cb_r,
    cc_s,
    cc_r,
    ha_s,
    ha_r,
):
    nz, nr, ng, chans, width, half = sizes
    ny = nr // ng
    z = lax.axis_index("chan")
    r = lax.axis_index("rad")
    g = lax.rem(r, ng)
    y = lax.div(r, ng)
    total_rows = width * nr
    delta = SPAN / total_rows

    def zdev(offset):
        return (lax.rem(z + offset + nz, nz), r)

    def gdev(k):
        return (z, y * ng + lax.rem(g + k, ng))

    def ydev(k):
        return (z, lax.rem(y + k, ny) * ng + g)

    load = pltpu.make_async_copy(
        wave_hbm, vbuf.at[0, :, :, pl.ds(LANES, width)], io_sem.at[0]
    )
    load.start()

    zeros_edge = jnp.zeros((chans, LANES), F32)
    for par in range(2):
        for p in range(2):
            vbuf[par, p, :, 0:LANES] = zeros_edge
            vbuf[par, p, :, LANES + width : 2 * LANES + width] = zeros_edge

    barrier = pltpu.get_barrier_semaphore()

    def greet(device):
        pl.semaphore_signal(barrier, inc=1, device_id=device, device_id_type=MESH)

    for k in range(1, nz):
        greet(zdev(k))
    for k in range(1, ng):
        greet(gdev(k))
    for k in range(1, ny):
        greet(ydev(k))
    greet((z, lax.rem(r + 1, nr)))
    greet((z, lax.rem(r + nr - 1, nr)))

    order = as_column(order_ref[...].astype(F32))
    ell = as_column(ell_ref[...].astype(F32))
    which = as_column(which_ref[...].astype(F32))
    strength = ell * (ell + 1.0)
    tiles = width // LANES
    for t in range(tiles):
        lane = lax.broadcasted_iota(jnp.int32, (1, LANES), 1)
        index = (r * width + t * LANES + lane).astype(F32)
        radius = 8.0 + 400.0 * (index + 0.5) / total_rows
        scaled = radius / 408.0
        logs = jnp.log(scaled)
        up = jnp.exp(order * logs)
        dn = 1.0 / (up * scaled)
        for mh in range(2):
            up_t[t, mh] = up[mh * half : (mh + 1) * half]
            dn_t[t, mh] = dn[mh * half : (mh + 1) * half]
        inv = 1.0 / (4.0 * radius * radius)
        lanes = slice(t * LANES, (t + 1) * LANES)
        for c0 in range(0, chans, ROWS_STEP):
            rows = slice(c0, c0 + ROWS_STEP)
            dg = 0.5 + strength[rows] * inv
            diag[rows, lanes] = dg
            scl[rows, lanes] = 1.0 / (1.0 + dg * dg)
            pick = which[rows]
            value = jnp.zeros((ROWS_STEP, LANES), F32)
            for o in range(orbitals_ref.shape[0]):
                value = jnp.where(pick == float(o), orbitals_ref[o : o + 1, lanes], value)
            orb[rows, lanes] = value
    hi, lo = split2(density_ref[...])
    d_hi[...] = hi
    d_lo[...] = lo
    hi, lo = split2(coupling_ref[...])
    f_hi[...] = hi
    f_lo[...] = lo
    rhs[...] = jnp.zeros_like(rhs)
    i0 = lax.broadcasted_iota(jnp.int32, (LANES, LANES), 0)
    i1 = lax.broadcasted_iota(jnp.int32, (LANES, LANES), 1)
    tri_in = jnp.where(i0 <= i1, 1.0, 0.0).astype(BF16)
    tri_out = jnp.where(i0 > i1, 1.0, 0.0).astype(BF16)
    j0 = lax.broadcasted_iota(jnp.int32, (32, 32), 0)
    j1 = lax.broadcasted_iota(jnp.int32, (32, 32), 1)
    same = (j0 // 4) == (j1 // 4)
    is_in2 = lax.rem(j0 // 4, 2) == 0
    group_sum = jnp.where(same, 1.0, 0.0).astype(F32)
    group_tri = jnp.where(
        same & ((is_in2 & (j1 < j0)) | (~is_in2 & (j1 > j0))), 1.0, 0.0
    ).astype(F32)
    row32 = lax.broadcasted_iota(jnp.int32, (32, LANES), 0)
    is_in = lax.rem(row32 // 4, 2) == 0
    lane_id = lax.broadcasted_iota(jnp.int32, (half, LANES), 1)

    load.wait()
    pl.semaphore_wait(barrier, (nz - 1) + (ng - 1) + (ny - 1) + 2)

    def rs_copy(pc, i):
        sign = 1 if pc == 0 else -1
        chunk, target = RS_PLAN[i]
        return pltpu.make_async_remote_copy(
            src_ref=rho.at[pc, lax.rem(z + sign * chunk + nz, nz)],
            dst_ref=rsbuf.at[pc, i],
            send_sem=rs_s.at[pc, i],
            recv_sem=rs_r.at[pc, i],
            device_id=zdev(sign * target),
            device_id_type=MESH,
        )

    def ag_copy(pc, i):
        sign = 1 if pc == 0 else -1
        chunk, target = AG_PLAN[i]
        owner = lax.rem(z + sign * chunk + nz, nz)
        return pltpu.make_async_remote_copy(
            src_ref=pot.at[pc, owner],
            dst_ref=pot.at[pc, owner],
            send_sem=ag_s.at[pc, i],
            recv_sem=ag_r.at[pc, i],
            device_id=zdev(sign * target),
            device_id_type=MESH,
        )

    def small_copy(src, buf, send, recv, par, k, device):
        return pltpu.make_async_remote_copy(
            src_ref=src,
            dst_ref=buf.at[par, k - 1],
            send_sem=send.at[k - 1],
            recv_sem=recv.at[par, k - 1],
            device_id=device,
            device_id_type=MESH,
        )

    def ca_copy(par, k):
        return small_copy(ca_src, ca_buf, ca_s, ca_r, par, k, gdev(k))

    def cb_copy(par, k):
        return small_copy(cb_src, cb_buf, cb_s, cb_r, par, k, ydev(k))

    def cc_copy(par, k):
        return small_copy(cc_src, cc_buf, cc_s, cc_r, par, k, zdev(k))

    def halo_copy(par, side):
        here, there = (width, 0) if side == 0 else (LANES, LANES + width)
        to = r + 1 if side == 0 else r - 1
        to = lax.rem(to + nr, nr)
        return pltpu.make_async_remote_copy(
            src_ref=vbuf.at[par, :, :, pl.ds(here, LANES)],
            dst_ref=vbuf.at[par, :, :, pl.ds(there, LANES)],
            send_sem=ha_s.at[side],
            recv_sem=ha_r.at[par, side],
            device_id=(z, to),
            device_id_type=MESH,
        )

    def densities(par, pc):
        base = pc * 2 * LANES
        for p in range(2):
            weighted = (
                vbuf[par, p, :, pl.ds(LANES + base, 2 * LANES)] * orb[:, base : base + 2 * LANES]
            )
            hi, lo = split2(weighted)
            part = dot(d_hi[...], hi) + (dot(d_hi[...], lo) + dot(d_lo[...], hi))
            for mh in range(2):
                for h in range(2):
                    rho[pc, 4 * p + 2 * mh + h] = part[
                        mh * half : (mh + 1) * half, h * LANES : (h + 1) * LANES
                    ]
        for i in range(5):
            rs_copy(pc, i).start()

    def totals(par):
        for mh in range(2):
            acc = jnp.zeros((half, LANES), F32)
            for p in range(2):
                for t in range(tiles):
                    block = rho[t // 2, 4 * p + 2 * mh + t % 2] * delta
                    for kind, table in ((0, up_t), (1, dn_t)):
                        s = jnp.sum(block * table[t, mh], axis=1, keepdims=True)
                        acc = jnp.where(lane_id == p * 8 + kind * 4 + t, s, acc)
            full = jnp.concatenate([acc, jnp.zeros((LANES - half, LANES), F32)], axis=0)
            ca_src[mh * 16 : (mh + 1) * 16, :] = jnp.transpose(full)[0:16]
        for k in range(1, ng):
            ca_copy(par, k).start()

        @pl.when(r < nr - 1)
        def _():
            halo_copy(par, 0).start()

        @pl.when(r > 0)
        def _():
            halo_copy(par, 1).start()

    def communicate(par):
        for pc in range(2):
            sign = 1 if pc == 0 else -1
            rs_copy(pc, 0).wait_recv()
            rs_copy(pc, 1).wait_recv()
            at = lax.rem(z - 2 * sign + nz, nz)
            rho[pc, at] = rho[pc, at] + rsbuf[pc, 0] + rsbuf[pc, 1]
            rs_copy(pc, 5).start()
            rs_copy(pc, 2).wait_recv()
            at = lax.rem(z + 2 * sign + nz, nz)
            rho[pc, at] = rho[pc, at] + rsbuf[pc, 2]
            rs_copy(pc, 6).start()
        below = jnp.zeros((32, LANES), F32)
        mine = ca_src[...]
        whole = mine
        for k in range(1, ng):
            ca_copy(par, k).wait_recv()
            peer = lax.rem(g - k + ng, ng)
            got = ca_buf[par, k - 1]
            w_in = jnp.where(peer < g, 1.0, 0.0).astype(F32)
            w_out = jnp.where(peer > g, 1.0, 0.0).astype(F32)
            below = below + got * jnp.where(is_in, w_in, w_out)
            whole = whole + got
        cb_src[...] = whole
        for k in range(1, ny):
            cb_copy(par, k).start()
        quarter = lax.rem(lax.div(z, 2), 2)
        for pc in range(2):
            for i in (3, 4, 5, 6):
                rs_copy(pc, i).wait_recv()
            acc = (rho[pc, z] + rsbuf[pc, 3]) + (rsbuf[pc, 4] + rsbuf[pc, 5]) + rsbuf[pc, 6]
            acc = acc * delta
            tile = 2 * pc + lax.rem(z, 2)
            up = up_t[tile, quarter]
            dn = dn_t[tile, quarter]

            def local(x, tri):
                hi = x.astype(BF16).astype(F32)
                both = jnp.concatenate([hi, x - hi], axis=0).astype(BF16)
                s = dot(both, tri)
                return s[:half] + s[half:]

            pot[pc, z] = dn * local(acc * up, tri_in) + up * local(acc * dn, tri_out)
            for i in range(4):
                ag_copy(pc, i).start()
        for k in range(1, ny):
            cb_copy(par, k).wait_recv()
            peer = lax.rem(y - k + ny, ny)
            w_in = jnp.where(peer < y, 1.0, 0.0).astype(F32)
            w_out = jnp.where(peer > y, 1.0, 0.0).astype(F32)
            below = below + cb_buf[par, k - 1] * jnp.where(is_in, w_in, w_out)
        carry = jnp.dot(
            group_sum, below, precision=lax.Precision.HIGHEST, preferred_element_type=F32
        ) + jnp.dot(group_tri, mine, precision=lax.Precision.HIGHEST, preferred_element_type=F32)
        cc_src[...] = carry
        for k in range(1, nz):
            cc_copy(par, k).start()
        for pc in range(2):
            ag_copy(pc, 0).wait_recv()
            ag_copy(pc, 4).start()
            ag_copy(pc, 5).start()
            ag_copy(pc, 1).wait_recv()
            ag_copy(pc, 6).start()
        for k in range(1, nz):
            cc_copy(par, k).wait_recv()
            carry = carry + cc_buf[par, k - 1]
        for pc in range(2):
            for i in range(7):
                rs_copy(pc, i).wait_send()
        for k in range(1, ng):
            ca_copy(par, k).wait_send()
        for k in range(1, ny):
            cb_copy(par, k).wait_send()
        for k in range(1, nz):
            cc_copy(par, k).wait_send()

        @pl.when(r < nr - 1)
        def _():
            halo_copy(par, 0).wait_send()
            halo_copy(par, 1).wait_recv()

        @pl.when(r > 0)
        def _():
            halo_copy(par, 1).wait_send()
            halo_copy(par, 0).wait_recv()

        pad = jnp.zeros((LANES - 16, LANES), F32)
        return [
            jnp.transpose(jnp.concatenate([carry[mh * 16 : (mh + 1) * 16], pad], axis=0))[:half]
            for mh in range(2)
        ]

    def advance(n, par, pc, carry):
        base = pc * 2 * LANES
        for i in (2, 3, 4, 5, 6):
            ag_copy(pc, i).wait_recv()
        for i in range(7):
            ag_copy(pc, i).wait_send()
        for p in range(2):
            cols = []
            for h in range(2):
                t = 2 * pc + h
                parts = []
                for mh in range(2):
                    k = p * 8 + t
                    parts.append(
                        pot[pc, 4 * p + 2 * mh + h]
                        + dn_t[t, mh] * carry[mh][:, k : k + 1]
                        + up_t[t, mh] * carry[mh][:, k + 4 : k + 5]
                    )
                cols.append(jnp.concatenate(parts, axis=0))
            hi, lo = split2(jnp.concatenate(cols, axis=1))
            field[p] = dot(f_hi[...], hi) + (dot(f_hi[...], lo) + dot(f_lo[...], hi))
        first = n == 0
        for c0 in range(0, chans, ROWS_STEP):
            rows = slice(c0, c0 + ROWS_STEP)
            lanes = slice(base, base + 2 * LANES)
            ob = orb[rows, lanes]
            v, w = [], []
            for p in range(2):
                x = vbuf[par, p, rows, pl.ds(base, 4 * LANES)]
                left = pltpu.roll(x, 1, 1)[:, LANES : 3 * LANES]
                right = pltpu.roll(x, 4 * LANES - 1, 1)[:, LANES : 3 * LANES]
                v.append(x[:, LANES : 3 * LANES])
                w.append(field[p, rows, :] * ob - 0.25 * (left + right))
            dg = diag[rows, lanes]
            r0 = jnp.where(first, v[0] + (w[1] + dg * v[1]), rhs[0, rows, lanes])
            r1 = jnp.where(first, v[1] - (w[0] + dg * v[0]), rhs[1, rows, lanes])
            rhs[0, rows, lanes] = r0
            rhs[1, rows, lanes] = r1
            n0 = r0 + w[1]
            n1 = r1 - w[0]
            sc = scl[rows, lanes]
            vbuf[1 - par, 0, rows, pl.ds(LANES + base, 2 * LANES)] = (n0 + dg * n1) * sc
            vbuf[1 - par, 1, rows, pl.ds(LANES + base, 2 * LANES)] = (n1 - dg * n0) * sc

    densities(0, 0)
    densities(0, 1)
    totals(0)

    def sweep(n, c):
        par = lax.rem(n, 2)
        carry = communicate(par)
        for pc in range(2):
            advance(n, par, pc, carry)

            @pl.when(n < SWEEPS - 1)
            def _():
                densities(1 - par, pc)

        @pl.when(n < SWEEPS - 1)
        def _():
            totals(1 - par)

        return c

    lax.fori_loop(0, SWEEPS, sweep, 0)
    store = pltpu.make_async_copy(
        vbuf.at[SWEEPS % 2, :, :, pl.ds(LANES, width)], out_hbm, io_sem.at[1]
    )
    store.start()
    store.wait()


def body(nz, nr, wavefunc, orbitals, channel_orbital, channel_l, row_order, density, coupling):
    chans, width = wavefunc.shape[1:]
    rows = row_order.shape[0]
    half = rows // 2
    ng = 8 if nr % 8 == 0 else 2
    ny = nr // ng
    vmem = pl.BlockSpec(memory_space=pltpu.VMEM)
    hbm = pl.BlockSpec(memory_space=pl.ANY)
    dma = pltpu.SemaphoreType.DMA
    scratch = [
        pltpu.VMEM((2, 2, chans, width + 2 * LANES), F32),
        pltpu.VMEM((2, chans, width), F32),
        pltpu.VMEM((chans, width), F32),
        pltpu.VMEM((chans, width), F32),
        pltpu.VMEM((chans, width), F32),
        pltpu.VMEM((2, chans, 2 * LANES), F32),
        pltpu.VMEM((4, 2, half, LANES), F32),
        pltpu.VMEM((4, 2, half, LANES), F32),
        pltpu.VMEM((rows, chans), BF16),
        pltpu.VMEM((rows, chans), BF16),
        pltpu.VMEM((chans, rows), BF16),
        pltpu.VMEM((chans, rows), BF16),
        pltpu.VMEM((2, 8, half, LANES), F32),
        pltpu.VMEM((2, 8, half, LANES), F32),
        pltpu.VMEM((2, 7, half, LANES), F32),
        pltpu.VMEM((32, LANES), F32),
        pltpu.VMEM((2, ng - 1, 32, LANES), F32),
        pltpu.VMEM((32, LANES), F32),
        pltpu.VMEM((2, ny - 1, 32, LANES), F32),
        pltpu.VMEM((32, LANES), F32),
        pltpu.VMEM((2, nz - 1, 32, LANES), F32),
        dma((2,)),
        dma((2, 7)),
        dma((2, 7)),
        dma((2, 7)),
        dma((2, 7)),
        dma((ng - 1,)),
        dma((2, ng - 1)),
        dma((ny - 1,)),
        dma((2, ny - 1)),
        dma((nz - 1,)),
        dma((2, nz - 1)),
        dma((2,)),
        dma((2, 2)),
    ]
    return pl.pallas_call(
        functools.partial(kernel, (nz, nr, ng, chans, width, half)),
        out_shape=jax.ShapeDtypeStruct(wavefunc.shape, F32),
        in_specs=[hbm] + [vmem] * 6,
        out_specs=hbm,
        scratch_shapes=scratch,
        compiler_params=pltpu.CompilerParams(
            collective_id=0, has_side_effects=True, vmem_limit_bytes=48 << 20
        ),
        name="cn_step",
    )(
        wavefunc,
        orbitals,
        channel_orbital.reshape(1, chans),
        channel_l.reshape(1, chans),
        row_order.reshape(1, rows),
        density,
        coupling,
    )


def solution(mesh):
    placed = (
        P(None, "chan", "rad"),
        P(None, "rad"),
        P("chan"),
        P("chan"),
        P(),
        P(None, "chan"),
        P("chan", None),
    )
    return jax.shard_map(
        functools.partial(body, mesh.shape["chan"], mesh.shape["rad"]),
        mesh=mesh,
        in_specs=placed,
        out_specs=P(None, "chan", "rad"),
        check_vma=False,
    )
```

```python
import functools

import jax
import jax.numpy as jnp
from jax import lax
from jax.experimental import pallas as pl
from jax.experimental.pallas import tpu as pltpu
from jax.sharding import PartitionSpec as P

SWEEPS = 4
MESH = pl.DeviceIdType.MESH
F32 = jnp.float32
BF16 = jnp.bfloat16
LANES = 128
SPAN = 400.0 / 408.0

RS_PLAN = ((-4, -2), (-3, -1), (3, 1), (-1, -1), (1, 1), (-2, -2), (2, 2))
AG_PLAN = ((0, 2), (0, -2), (0, 1), (0, -1), (-2, 2), (-2, 1), (2, -1))
PARTS = ((0, 40), (40, 32))
ROWS_STEP = 32


def split2(x):
    hi = x.astype(BF16)
    return hi, (x - hi.astype(F32)).astype(BF16)


def dot(a, b):
    return jnp.dot(a, b, preferred_element_type=F32)


def as_column(row):
    eight = jnp.broadcast_to(row, (8, row.shape[1]))
    first = lax.broadcasted_iota(jnp.int32, (8, LANES), 0) == 0
    return lax.dot_general(
        eight,
        jnp.where(first, 1.0, 0.0).astype(F32),
        (((0,), (0,)), ((), ())),
        precision=lax.Precision.HIGHEST,
        preferred_element_type=F32,
    )


def kernel(
    sizes,
    wave_hbm,
    orbitals_ref,
    which_ref,
    ell_ref,
    order_ref,
    density_ref,
    coupling_ref,
    out_hbm,
    vbuf,
    rhs,
    orb,
    diag,
    scl,
    field,
    up_t,
    dn_t,
    d_hi,
    d_lo,
    f_hi,
    f_lo,
    rho,
    pot,
    rsbuf,
    own,
    tin01,
    sc_in,
    sc_out,
    ca_src,
    ca_buf,
    cb_src,
    cb_buf,
    cc_src,
    cc_buf,
    io_sem,
    rs_s,
    rs_r,
    ag_s,
    ag_r,
    ca_s,
    ca_r,
    cb_s,
    cb_r,
    cc_s,
    cc_r,
    ha_s,
    ha_r,
):
    nz, nr, ng, chans, width, half = sizes
    ny = nr // ng
    z = lax.axis_index("chan")
    r = lax.axis_index("rad")
    g = lax.rem(r, ng)
    y = lax.div(r, ng)
    total_rows = width * nr
    delta = SPAN / total_rows

    def zdev(offset):
        return (lax.rem(z + offset + nz, nz), r)

    sign = 1 - 2 * lax.rem(r, 2)

    def near(offset):
        return lax.rem(z + sign * offset + nz, nz)

    def gdev(k):
        return (z, y * ng + lax.rem(g + k, ng))

    def ydev(k):
        return (z, lax.rem(y + k, ny) * ng + g)

    load = pltpu.make_async_copy(
        wave_hbm, vbuf.at[0, :, :, pl.ds(LANES, width)], io_sem.at[0]
    )
    load.start()

    zeros_edge = jnp.zeros((chans, LANES), F32)
    for par in range(2):
        for p in range(2):
            vbuf[par, p, :, 0:LANES] = zeros_edge
            vbuf[par, p, :, LANES + width : 2 * LANES + width] = zeros_edge

    barrier = pltpu.get_barrier_semaphore()

    def greet(device):
        pl.semaphore_signal(barrier, inc=1, device_id=device, device_id_type=MESH)

    for k in (1, 2, nz - 2, nz - 1):
        greet(zdev(k))
    for k in range(1, ng):
        greet(gdev(k))
    for k in range(1, ny):
        greet(ydev(k))

    tiles = width // LANES
    i0 = lax.broadcasted_iota(jnp.int32, (LANES, LANES), 0)
    i1 = lax.broadcasted_iota(jnp.int32, (LANES, LANES), 1)
    tri_in = jnp.where(i0 <= i1, 1.0, 0.0).astype(BF16)
    tri_out = jnp.where(i0 > i1, 1.0, 0.0).astype(BF16)
    lane_id = lax.broadcasted_iota(jnp.int32, (half, LANES), 1)

    def spread_orbitals():
        which = as_column(which_ref[...].astype(F32))
        for t in range(tiles):
            lanes = slice(t * LANES, (t + 1) * LANES)
            for c0 in range(0, chans, ROWS_STEP):
                rows = slice(c0, c0 + ROWS_STEP)
                pick = which[rows]
                value = jnp.zeros((ROWS_STEP, LANES), F32)
                for o in range(orbitals_ref.shape[0]):
                    value = jnp.where(pick == float(o), orbitals_ref[o : o + 1, lanes], value)
                orb[rows, lanes] = value
        hi, lo = split2(density_ref[...])
        d_hi[...] = hi
        d_lo[...] = lo

    def radius_of(t):
        lane = lax.broadcasted_iota(jnp.int32, (1, LANES), 1)
        index = (r * width + t * LANES + lane).astype(F32)
        return 8.0 + 400.0 * (index + 0.5) / total_rows

    def power_tables():
        order = as_column(order_ref[...].astype(F32))
        for t in range(tiles):
            scaled = radius_of(t) / 408.0
            up = jnp.exp(order * jnp.log(scaled))
            dn = 1.0 / (up * scaled)
            inv_dn = jnp.broadcast_to((up * scaled)[:, LANES - 1 :], up.shape)
            inv_up = jnp.broadcast_to((dn * scaled)[:, :1], up.shape)
            for mh in range(2):
                rows = slice(mh * half, (mh + 1) * half)
                up_t[t, mh] = up[rows]
                dn_t[t, mh] = dn[rows]
                sc_in[t, mh] = inv_dn[rows]
                sc_out[t, mh] = inv_up[rows]

    def diagonal_tables():
        ell = as_column(ell_ref[...].astype(F32))
        strength = ell * (ell + 1.0)
        for t in range(tiles):
            radius = radius_of(t)
            inv = 1.0 / (4.0 * radius * radius)
            lanes = slice(t * LANES, (t + 1) * LANES)
            for c0 in range(0, chans, ROWS_STEP):
                rows = slice(c0, c0 + ROWS_STEP)
                dg = 0.5 + strength[rows] * inv
                diag[rows, lanes] = dg
                scl[rows, lanes] = 1.0 / (1.0 + dg * dg)
        turned = jnp.concatenate(
            [coupling_ref[...], jnp.zeros((chans - 2 * half, chans), F32)], axis=0
        )
        hi, lo = split2(jnp.transpose(turned)[:, : 2 * half])
        f_hi[...] = hi
        f_lo[...] = lo
        rhs[...] = jnp.zeros_like(rhs)

    def rs_copy(pc, part, i):
        chunk, target = RS_PLAN[i]
        rows = pl.ds(*PARTS[part])
        return pltpu.make_async_remote_copy(
            src_ref=rho.at[pc, near(chunk), rows],
            dst_ref=rsbuf.at[pc, i, rows],
            send_sem=rs_s.at[pc, part, i],
            recv_sem=rs_r.at[pc, part, i],
            device_id=(near(target), r),
            device_id_type=MESH,
        )

    def ag_copy(pc, part, i):
        chunk, target = AG_PLAN[i]
        place = pot.at[pc, near(chunk), pl.ds(*PARTS[part])]
        return pltpu.make_async_remote_copy(
            src_ref=place,
            dst_ref=place,
            send_sem=ag_s.at[pc, part, i],
            recv_sem=ag_r.at[pc, part, i],
            device_id=(near(target), r),
            device_id_type=MESH,
        )

    def small_copy(src, buf, send, recv, par, k, device):
        return pltpu.make_async_remote_copy(
            src_ref=src,
            dst_ref=buf.at[par, k - 1],
            send_sem=send.at[k - 1],
            recv_sem=recv.at[par, k - 1],
            device_id=device,
            device_id_type=MESH,
        )

    def ca_copy(par, k):
        return small_copy(ca_src, ca_buf, ca_s, ca_r, par, k, gdev(k))

    def cb_copy(par, k):
        return small_copy(cb_src, cb_buf, cb_s, cb_r, par, k, ydev(k))

    def cc_copy(par, k):
        return small_copy(cc_src, cc_buf, cc_s, cc_r, par, k, zdev(k))

    def halo_copy(par, side):
        here, there = (width, 0) if side == 0 else (LANES, LANES + width)
        to = r + 1 if side == 0 else r - 1
        to = lax.rem(to + nr, nr)
        return pltpu.make_async_remote_copy(
            src_ref=vbuf.at[par, :, :, pl.ds(here, LANES)],
            dst_ref=vbuf.at[par, :, :, pl.ds(there, LANES)],
            send_sem=ha_s.at[side],
            recv_sem=ha_r.at[par, side],
            device_id=(z, to),
            device_id_type=MESH,
        )

    def densities(par, pc):
        base = pc * 2 * LANES
        for p in range(2):
            weighted = (
                vbuf[par, p, :, pl.ds(LANES + base, 2 * LANES)] * orb[:, base : base + 2 * LANES]
            )
            hi, lo = split2(weighted)
            part = dot(d_hi[...], hi) + (dot(d_hi[...], lo) + dot(d_lo[...], hi))
            for mh in range(2):
                for h in range(2):
                    rho[pc, 4 * p + 2 * mh + h] = part[
                        mh * half : (mh + 1) * half, h * LANES : (h + 1) * LANES
                    ]

    def send_far(pc):
        for part in range(len(PARTS)):
            for i in (0, 1, 2):
                rs_copy(pc, part, i).start()

    def send_direct():
        for pc in range(2):
            for part in range(len(PARTS)):
                for i in (3, 4):
                    rs_copy(pc, part, i).start()

    def totals(par):
        acc = jnp.zeros((half, LANES), F32)
        for p in range(2):
            for mh in range(2):
                blocks = [rho[t // 2, 4 * p + 2 * mh + t % 2] * delta for t in range(tiles)]
                ups = [blocks[t] * up_t[t, mh] for t in range(tiles)]
                dns = [blocks[t] * dn_t[t, mh] for t in range(tiles)]
                near_out = dns[0] + dns[1]
                far_out = dns[2] + dns[3]
                sums = ((ups[0] + ups[1]) + (ups[2] + ups[3]), near_out + far_out, far_out)
                for kind in range(3):
                    s = jnp.sum(sums[kind], axis=1, keepdims=True)
                    acc = jnp.where(lane_id == kind * 4 + p * 2 + mh, s, acc)
        full = jnp.concatenate([acc, jnp.zeros((LANES - half, LANES), F32)], axis=0)
        own[...] = jnp.transpose(full)[0:16]
        ca_src[0] = own[0:4]
        ca_src[1] = own[4:8]
        for k in range(1, ng):
            ca_copy(par, k).start()

    def communicate(par):
        for pc in range(2):
            for part in range(len(PARTS)):
                rows = pl.ds(*PARTS[part])
                rs_copy(pc, part, 0).wait_recv()
                rs_copy(pc, part, 1).wait_recv()
                at = near(-2)
                rho[pc, at, rows] = rho[pc, at, rows] + rsbuf[pc, 0, rows] + rsbuf[pc, 1, rows]
                rs_copy(pc, part, 5).start()
                rs_copy(pc, part, 2).wait_recv()
                at = near(2)
                rho[pc, at, rows] = rho[pc, at, rows] + rsbuf[pc, 2, rows]
                rs_copy(pc, part, 6).start()
        below = jnp.zeros((4, LANES), F32)
        above = jnp.zeros((4, LANES), F32)
        whole_in = ca_src[0]
        whole_out = ca_src[1]
        for k in range(1, ng):
            ca_copy(par, k).wait_recv()
            peer = lax.rem(g - k + ng, ng)
            got_in = ca_buf[par, k - 1, 0]
            got_out = ca_buf[par, k - 1, 1]
            below = below + got_in * jnp.where(peer < g, 1.0, 0.0).astype(F32)
            above = above + got_out * jnp.where(peer > g, 1.0, 0.0).astype(F32)
            whole_in = whole_in + got_in
            whole_out = whole_out + got_out
        cb_src[0] = whole_in
        cb_src[1] = whole_out
        for k in range(1, ny):
            cb_copy(par, k).start()

        @pl.when(r < nr - 1)
        def _():
            halo_copy(par, 0).start()

        @pl.when(r > 0)
        def _():
            halo_copy(par, 1).start()

        quarter = lax.rem(lax.div(z, 2), 2)
        for pc in range(2):
            tile = 2 * pc + lax.rem(z, 2)
            for part in range(len(PARTS)):
                size = PARTS[part][1]
                rows = pl.ds(*PARTS[part])
                for i in (3, 4, 5, 6):
                    rs_copy(pc, part, i).wait_recv()
                acc = (rho[pc, z, rows] + rsbuf[pc, 3, rows]) + (
                    rsbuf[pc, 4, rows] + rsbuf[pc, 5, rows]
                )
                acc = (acc + rsbuf[pc, 6, rows]) * delta
                up = up_t[tile, quarter, rows]
                dn = dn_t[tile, quarter, rows]

                def local(x, tri):
                    hi = x.astype(BF16).astype(F32)
                    both = jnp.concatenate([hi, x - hi], axis=0).astype(BF16)
                    s = dot(both, tri)
                    return s[:size] + s[size:]

                pot[pc, z, rows] = dn * local(acc * up, tri_in) + up * local(acc * dn, tri_out)
                for i in range(4):
                    ag_copy(pc, part, i).start()
        for k in range(1, ny):
            cb_copy(par, k).wait_recv()
            peer = lax.rem(y - k + ny, ny)
            below = below + cb_buf[par, k - 1, 0] * jnp.where(peer < y, 1.0, 0.0).astype(F32)
            above = above + cb_buf[par, k - 1, 1] * jnp.where(peer > y, 1.0, 0.0).astype(F32)
        cc_src[0] = below
        cc_src[1] = above + own[8:12]
        cc_src[2] = above
        for k in range(1, nz):
            cc_copy(par, k).start()
        for pc in range(2):
            for part in range(len(PARTS)):
                ag_copy(pc, part, 0).wait_recv()
                ag_copy(pc, part, 4).start()
                ag_copy(pc, part, 5).start()
                ag_copy(pc, part, 1).wait_recv()
                ag_copy(pc, part, 6).start()
        carry = [cc_src[kind] for kind in range(3)]
        for k in range(1, nz):
            cc_copy(par, k).wait_recv()
            carry = [carry[kind] + cc_buf[par, k - 1, kind] for kind in range(3)]
        for pc in range(2):
            for part in range(len(PARTS)):
                for i in range(7):
                    rs_copy(pc, part, i).wait_send()
        for k in range(1, ng):
            ca_copy(par, k).wait_send()
        for k in range(1, ny):
            cb_copy(par, k).wait_send()
        for k in range(1, nz):
            cc_copy(par, k).wait_send()

        @pl.when(r < nr - 1)
        def _():
            halo_copy(par, 0).wait_send()
            halo_copy(par, 1).wait_recv()

        @pl.when(r > 0)
        def _():
            halo_copy(par, 1).wait_send()
            halo_copy(par, 0).wait_recv()

        for kind in range(3):
            own[4 * kind : 4 * kind + 4] = carry[kind]
        pad = jnp.zeros((LANES - 16, LANES), F32)
        return jnp.transpose(jnp.concatenate([own[...], pad], axis=0))[:half]

    def advance(n, par, pc, carry):
        base = pc * 2 * LANES
        for part in range(len(PARTS)):
            for i in (2, 3, 4, 5, 6):
                ag_copy(pc, part, i).wait_recv()
            for i in range(7):
                ag_copy(pc, part, i).wait_send()
        for p in range(2):
            cols = [[], []]
            for mh in range(2):
                k = 2 * p + mh
                t = 2 * pc
                first_pot = pot[pc, 4 * p + 2 * mh]
                second_pot = pot[pc, 4 * p + 2 * mh + 1]
                wide = (half, LANES)
                below = jnp.broadcast_to(carry[:, k : k + 1], wide)
                at = 4 * (pc + 1) + k
                above = jnp.broadcast_to(carry[:, at : at + 1], wide)
                in_first = jnp.broadcast_to(first_pot[:, LANES - 1 :], wide) * sc_in[t, mh]
                out_second = jnp.broadcast_to(second_pot[:, :1], wide) * sc_out[t + 1, mh]
                if pc == 0:
                    in_second = jnp.broadcast_to(second_pot[:, LANES - 1 :], wide)
                    tin01[k] = in_first + in_second * sc_in[t + 1, mh]
                else:
                    below = below + tin01[k]
                cols[0].append(
                    first_pot + dn_t[t, mh] * below + up_t[t, mh] * (above + out_second)
                )
                cols[1].append(
                    second_pot + dn_t[t + 1, mh] * (below + in_first) + up_t[t + 1, mh] * above
                )
            cols = [jnp.concatenate(parts, axis=0) for parts in cols]
            hi, lo = split2(jnp.concatenate(cols, axis=1))
            field[p] = dot(f_hi[...], hi) + (dot(f_hi[...], lo) + dot(f_lo[...], hi))
        first = n == 0
        for c0 in range(0, chans, ROWS_STEP):
            rows = slice(c0, c0 + ROWS_STEP)
            lanes = slice(base, base + 2 * LANES)
            ob = orb[rows, lanes]
            v, w = [], []
            for p in range(2):
                x = vbuf[par, p, rows, pl.ds(base, 4 * LANES)]
                left = pltpu.roll(x, 1, 1)[:, LANES : 3 * LANES]
                right = pltpu.roll(x, 4 * LANES - 1, 1)[:, LANES : 3 * LANES]
                v.append(x[:, LANES : 3 * LANES])
                w.append(field[p, rows, :] * ob - 0.25 * (left + right))
            dg = diag[rows, lanes]
            r0 = jnp.where(first, v[0] + (w[1] + dg * v[1]), rhs[0, rows, lanes])
            r1 = jnp.where(first, v[1] - (w[0] + dg * v[0]), rhs[1, rows, lanes])
            rhs[0, rows, lanes] = r0
            rhs[1, rows, lanes] = r1
            n0 = r0 + w[1]
            n1 = r1 - w[0]
            sc = scl[rows, lanes]
            vbuf[1 - par, 0, rows, pl.ds(LANES + base, 2 * LANES)] = (n0 + dg * n1) * sc
            vbuf[1 - par, 1, rows, pl.ds(LANES + base, 2 * LANES)] = (n1 - dg * n0) * sc

    spread_orbitals()
    load.wait()
    densities(0, 0)
    pl.semaphore_wait(barrier, 4 + (ng - 1) + (ny - 1))
    send_far(0)
    densities(0, 1)
    send_far(1)
    send_direct()
    power_tables()
    totals(0)
    diagonal_tables()

    def store(pc):
        at = pc * 2 * LANES
        return pltpu.make_async_copy(
            vbuf.at[SWEEPS % 2, :, :, pl.ds(LANES + at, 2 * LANES)],
            out_hbm.at[:, :, pl.ds(at, 2 * LANES)],
            io_sem.at[pc],
        )

    def sweep(n, c):
        par = lax.rem(n, 2)
        carry = communicate(par)
        for pc in range(2):
            advance(n, par, pc, carry)

            @pl.when(n < SWEEPS - 1)
            def _():
                densities(1 - par, pc)
                send_far(pc)

            @pl.when(n == SWEEPS - 1)
            def _():
                store(pc).start()

        @pl.when(n < SWEEPS - 1)
        def _():
            send_direct()
            totals(1 - par)

        return c

    lax.fori_loop(0, SWEEPS, sweep, 0)
    for pc in range(2):
        store(pc).wait()


def body(nz, nr, wavefunc, orbitals, channel_orbital, channel_l, row_order, density, coupling):
    chans, width = wavefunc.shape[1:]
    rows = row_order.shape[0]
    half = rows // 2
    ng = 8 if nr % 8 == 0 else 2
    ny = nr // ng
    vmem = pl.BlockSpec(memory_space=pltpu.VMEM)
    hbm = pl.BlockSpec(memory_space=pl.ANY)
    dma = pltpu.SemaphoreType.DMA
    scratch = [
        pltpu.VMEM((2, 2, chans, width + 2 * LANES), F32),
        pltpu.VMEM((2, chans, width), F32),
        pltpu.VMEM((chans, width), F32),
        pltpu.VMEM((chans, width), F32),
        pltpu.VMEM((chans, width), F32),
        pltpu.VMEM((2, chans, 2 * LANES), F32),
        pltpu.VMEM((4, 2, half, LANES), F32),
        pltpu.VMEM((4, 2, half, LANES), F32),
        pltpu.VMEM((rows, chans), BF16),
        pltpu.VMEM((rows, chans), BF16),
        pltpu.VMEM((chans, rows), BF16),
        pltpu.VMEM((chans, rows), BF16),
        pltpu.VMEM((2, 8, half, LANES), F32),
        pltpu.VMEM((2, 8, half, LANES), F32),
        pltpu.VMEM((2, 7, half, LANES), F32),
        pltpu.VMEM((16, LANES), F32),
        pltpu.VMEM((4, half, LANES), F32),
        pltpu.VMEM((4, 2, half, LANES), F32),
        pltpu.VMEM((4, 2, half, LANES), F32),
        pltpu.VMEM((2, 4, LANES), F32),
        pltpu.VMEM((2, ng - 1, 2, 4, LANES), F32),
        pltpu.VMEM((2, 4, LANES), F32),
        pltpu.VMEM((2, ny - 1, 2, 4, LANES), F32),
        pltpu.VMEM((3, 4, LANES), F32),
        pltpu.VMEM((2, nz - 1, 3, 4, LANES), F32),
        dma((2,)),
        dma((2, len(PARTS), 7)),
        dma((2, len(PARTS), 7)),
        dma((2, len(PARTS), 7)),
        dma((2, len(PARTS), 7)),
        dma((ng - 1,)),
        dma((2, ng - 1)),
        dma((ny - 1,)),
        dma((2, ny - 1)),
        dma((nz - 1,)),
        dma((2, nz - 1)),
        dma((2,)),
        dma((2, 2)),
    ]
    return pl.pallas_call(
        functools.partial(kernel, (nz, nr, ng, chans, width, half)),
        out_shape=jax.ShapeDtypeStruct(wavefunc.shape, F32),
        in_specs=[hbm] + [vmem] * 6,
        out_specs=hbm,
        scratch_shapes=scratch,
        compiler_params=pltpu.CompilerParams(
            collective_id=0, has_side_effects=True, vmem_limit_bytes=48 << 20
        ),
        name="cn_step",
    )(
        wavefunc,
        orbitals,
        channel_orbital.reshape(1, chans),
        channel_l.reshape(1, chans),
        row_order.reshape(1, rows),
        density,
        coupling.T,
    )


def solution(mesh):
    placed = (
        P(None, "chan", "rad"),
        P(None, "rad"),
        P("chan"),
        P("chan"),
        P(),
        P(None, "chan"),
        P("chan", None),
    )
    return jax.shard_map(
        functools.partial(body, mesh.shape["chan"], mesh.shape["rad"]),
        mesh=mesh,
        in_specs=placed,
        out_specs=P(None, "chan", "rad"),
        check_vma=False,
    )
```

```python
import functools

import jax
import jax.numpy as jnp
from jax import lax
from jax.experimental import pallas as pl
from jax.experimental.pallas import tpu as pltpu
from jax.sharding import PartitionSpec as P

SWEEPS = 4
MESH = pl.DeviceIdType.MESH
F32 = jnp.float32
BF16 = jnp.bfloat16
LANES = 128
SPAN = 400.0 / 408.0

RS_PLAN = ((-4, -2), (-3, -1), (3, 1), (-1, -1), (1, 1), (-2, -2), (2, 2))
AG_PLAN = ((0, 2), (0, -2), (0, 1), (0, -1), (-2, 2), (-2, 1), (2, -1))
PARTS = ((0, 40), (40, 32))
ROWS_STEP = 32


def split2(x):
    hi = x.astype(BF16)
    return hi, (x - hi.astype(F32)).astype(BF16)


def dot(a, b):
    return jnp.dot(a, b, preferred_element_type=F32)


def as_column(row):
    eight = jnp.broadcast_to(row, (8, row.shape[1]))
    first = lax.broadcasted_iota(jnp.int32, (8, LANES), 0) == 0
    return lax.dot_general(
        eight,
        jnp.where(first, 1.0, 0.0).astype(F32),
        (((0,), (0,)), ((), ())),
        precision=lax.Precision.HIGHEST,
        preferred_element_type=F32,
    )


def kernel(
    sizes,
    wave_hbm,
    orbitals_ref,
    which_ref,
    ell_ref,
    order_ref,
    density_ref,
    coupling_ref,
    out_hbm,
    vbuf,
    rhs,
    orb,
    diag,
    scl,
    known,
    alpha,
    beta,
    field,
    w_hi,
    w_lo,
    up_t,
    dn_t,
    d_both,
    f_both,
    rho,
    pot,
    rsbuf,
    own,
    tin01,
    sc_in,
    sc_out,
    ca_src,
    ca_buf,
    cb_src,
    cb_buf,
    cc_src,
    cc_buf,
    io_sem,
    rs_s,
    rs_r,
    ag_s,
    ag_r,
    ca_s,
    ca_r,
    cb_s,
    cb_r,
    cc_s,
    cc_r,
    ha_s,
    ha_r,
):
    nz, nr, ng, chans, width, half = sizes
    ny = nr // ng
    z = lax.axis_index("chan")
    r = lax.axis_index("rad")
    g = lax.rem(r, ng)
    y = lax.div(r, ng)
    total_rows = width * nr
    delta = SPAN / total_rows

    def zdev(offset):
        return (lax.rem(z + offset + nz, nz), r)

    sign = 1 - 2 * lax.rem(r, 2)

    def near(offset):
        return lax.rem(z + sign * offset + nz, nz)

    def gdev(k):
        return (z, y * ng + lax.rem(g + k, ng))

    def ydev(k):
        return (z, lax.rem(y + k, ny) * ng + g)

    load = pltpu.make_async_copy(
        wave_hbm, vbuf.at[0, :, :, pl.ds(LANES, width)], io_sem.at[0]
    )
    load.start()

    zeros_edge = jnp.zeros((chans, LANES), F32)
    for par in range(2):
        for p in range(2):
            vbuf[par, p, :, 0:LANES] = zeros_edge
            vbuf[par, p, :, LANES + width : 2 * LANES + width] = zeros_edge

    barrier = pltpu.get_barrier_semaphore()

    def greet(device):
        pl.semaphore_signal(barrier, inc=1, device_id=device, device_id_type=MESH)

    for k in (1, 2, nz - 2, nz - 1):
        greet(zdev(k))
    for k in range(1, ng):
        greet(gdev(k))
    for k in range(1, ny):
        greet(ydev(k))

    tiles = width // LANES
    i0 = lax.broadcasted_iota(jnp.int32, (LANES, LANES), 0)
    i1 = lax.broadcasted_iota(jnp.int32, (LANES, LANES), 1)
    tri_in = jnp.where(i0 <= i1, 1.0, 0.0).astype(BF16)
    tri_out = jnp.where(i0 > i1, 1.0, 0.0).astype(BF16)
    lane_id = lax.broadcasted_iota(jnp.int32, (half, LANES), 1)

    def spread_orbitals():
        which = as_column(which_ref[...].astype(F32))
        for t in range(tiles):
            lanes = slice(t * LANES, (t + 1) * LANES)
            for c0 in range(0, chans, ROWS_STEP):
                rows = slice(c0, c0 + ROWS_STEP)
                pick = which[rows]
                value = jnp.zeros((ROWS_STEP, LANES), F32)
                for o in range(orbitals_ref.shape[0]):
                    value = jnp.where(pick == float(o), orbitals_ref[o : o + 1, lanes], value)
                orb[rows, lanes] = value
        hi, lo = split2(density_ref[...])
        d_both[: 2 * half] = hi
        d_both[2 * half :] = lo

    def radius_of(t):
        lane = lax.broadcasted_iota(jnp.int32, (1, LANES), 1)
        index = (r * width + t * LANES + lane).astype(F32)
        return 8.0 + 400.0 * (index + 0.5) / total_rows

    def power_tables():
        order = as_column(order_ref[...].astype(F32))
        for t in range(tiles):
            scaled = radius_of(t) / 408.0
            up = jnp.exp(order * jnp.log(scaled))
            dn = 1.0 / (up * scaled)
            inv_dn = jnp.broadcast_to((up * scaled)[:, LANES - 1 :], up.shape)
            inv_up = jnp.broadcast_to((dn * scaled)[:, :1], up.shape)
            for mh in range(2):
                rows = slice(mh * half, (mh + 1) * half)
                up_t[t, mh] = up[rows]
                dn_t[t, mh] = dn[rows]
                sc_in[t, mh] = inv_dn[rows]
                sc_out[t, mh] = inv_up[rows]

    def diagonal_tables():
        ell = as_column(ell_ref[...].astype(F32))
        strength = ell * (ell + 1.0)
        for t in range(tiles):
            radius = radius_of(t)
            inv = 1.0 / (4.0 * radius * radius)
            lanes = slice(t * LANES, (t + 1) * LANES)
            for c0 in range(0, chans, ROWS_STEP):
                rows = slice(c0, c0 + ROWS_STEP)
                dg = 0.5 + strength[rows] * inv
                sc = 1.0 / (1.0 + dg * dg)
                al = sc * orb[rows, lanes]
                diag[rows, lanes] = dg
                scl[rows, lanes] = sc
                alpha[rows, lanes] = al
                beta[rows, lanes] = al * dg
        turned = jnp.concatenate(
            [coupling_ref[...], jnp.zeros((chans - 2 * half, chans), F32)], axis=0
        )
        hi, lo = split2(jnp.transpose(turned)[:, : 2 * half])
        f_both[:chans] = hi
        f_both[chans:] = lo

    def rs_copy(pc, part, i):
        chunk, target = RS_PLAN[i]
        rows = pl.ds(*PARTS[part])
        return pltpu.make_async_remote_copy(
            src_ref=rho.at[pc, near(chunk), rows],
            dst_ref=rsbuf.at[pc, i, rows],
            send_sem=rs_s.at[pc, part, i],
            recv_sem=rs_r.at[pc, part, i],
            device_id=(near(target), r),
            device_id_type=MESH,
        )

    def ag_copy(pc, part, i):
        chunk, target = AG_PLAN[i]
        place = pot.at[pc, near(chunk), pl.ds(*PARTS[part])]
        return pltpu.make_async_remote_copy(
            src_ref=place,
            dst_ref=place,
            send_sem=ag_s.at[pc, part, i],
            recv_sem=ag_r.at[pc, part, i],
            device_id=(near(target), r),
            device_id_type=MESH,
        )

    def small_copy(src, buf, send, recv, par, k, device):
        return pltpu.make_async_remote_copy(
            src_ref=src,
            dst_ref=buf.at[par, k - 1],
            send_sem=send.at[k - 1],
            recv_sem=recv.at[par, k - 1],
            device_id=device,
            device_id_type=MESH,
        )

    def ca_copy(par, k):
        return small_copy(ca_src, ca_buf, ca_s, ca_r, par, k, gdev(k))

    def cb_copy(par, k):
        return small_copy(cb_src, cb_buf, cb_s, cb_r, par, k, ydev(k))

    def cc_copy(par, k):
        return small_copy(cc_src, cc_buf, cc_s, cc_r, par, k, zdev(k))

    def halo_copy(par, side):
        here, there = (width, 0) if side == 0 else (LANES, LANES + width)
        to = r + 1 if side == 0 else r - 1
        to = lax.rem(to + nr, nr)
        return pltpu.make_async_remote_copy(
            src_ref=vbuf.at[par, :, :, pl.ds(here, LANES)],
            dst_ref=vbuf.at[par, :, :, pl.ds(there, LANES)],
            send_sem=ha_s.at[side],
            recv_sem=ha_r.at[par, side],
            device_id=(z, to),
            device_id_type=MESH,
        )

    def weigh(par, pc):
        lanes = slice(pc * 2 * LANES, (pc + 1) * 2 * LANES)
        for c0 in range(0, chans, ROWS_STEP):
            rows = slice(c0, c0 + ROWS_STEP)
            for p in range(2):
                v = vbuf[par, p, rows, LANES + lanes.start : LANES + lanes.stop]
                hi, lo = split2(v * orb[rows, lanes])
                w_hi[p, rows] = hi
                w_lo[p, rows] = lo

    def densities(pc):
        rows = 2 * half
        for p in range(2):
            wide = dot(d_both[...], w_hi[p])
            part = wide[:rows] + (wide[rows:] + dot(d_both[:rows], w_lo[p]))
            for mh in range(2):
                for h in range(2):
                    rho[pc, 4 * p + 2 * mh + h] = part[
                        mh * half : (mh + 1) * half, h * LANES : (h + 1) * LANES
                    ]

    def prepare(n, par, pc):
        base = pc * 2 * LANES
        lanes = slice(base, base + 2 * LANES)

        def kinetic(rows):
            v, kin = [], []
            for p in range(2):
                x = vbuf[par, p, rows, pl.ds(base, 4 * LANES)]
                left = pltpu.roll(x, 1, 1)[:, LANES : 3 * LANES]
                right = pltpu.roll(x, 4 * LANES - 1, 1)[:, LANES : 3 * LANES]
                v.append(x[:, LANES : 3 * LANES])
                kin.append(-0.25 * (left + right))
            return v, kin

        @pl.when(n == 0)
        def _():
            for c0 in range(0, chans, ROWS_STEP):
                rows = slice(c0, c0 + ROWS_STEP)
                v, kin = kinetic(rows)
                dg = diag[rows, lanes]
                rhs[0, rows, lanes] = v[0] + (kin[1] + dg * v[1])
                rhs[1, rows, lanes] = v[1] - (kin[0] + dg * v[0])

        @pl.when(n == 1)
        def _():
            for c0 in range(0, chans, ROWS_STEP):
                rows = slice(c0, c0 + ROWS_STEP)
                ob = orb[rows, lanes]
                rhs[0, rows, lanes] = rhs[0, rows, lanes] + field[pc, 1, rows] * ob
                rhs[1, rows, lanes] = rhs[1, rows, lanes] - field[pc, 0, rows] * ob

        for c0 in range(0, chans, ROWS_STEP):
            rows = slice(c0, c0 + ROWS_STEP)
            v, kin = kinetic(rows)
            dg = diag[rows, lanes]
            sc = scl[rows, lanes]
            q0 = rhs[0, rows, lanes] + kin[1]
            q1 = rhs[1, rows, lanes] - kin[0]
            known[0, rows, lanes] = (q0 + dg * q1) * sc
            known[1, rows, lanes] = (q1 - dg * q0) * sc

    def send_far(pc):
        for part in range(len(PARTS)):
            for i in (0, 1, 2):
                rs_copy(pc, part, i).start()

    def send_direct(pc):
        for part in range(len(PARTS)):
            for i in (3, 4):
                rs_copy(pc, part, i).start()

    def totals(par):
        acc = jnp.zeros((half, LANES), F32)
        for p in range(2):
            for mh in range(2):
                blocks = [rho[t // 2, 4 * p + 2 * mh + t % 2] * delta for t in range(tiles)]
                ups = [blocks[t] * up_t[t, mh] for t in range(tiles)]
                dns = [blocks[t] * dn_t[t, mh] for t in range(tiles)]
                near_out = dns[0] + dns[1]
                far_out = dns[2] + dns[3]
                sums = ((ups[0] + ups[1]) + (ups[2] + ups[3]), near_out + far_out, far_out)
                for kind in range(3):
                    s = jnp.sum(sums[kind], axis=1, keepdims=True)
                    acc = jnp.where(lane_id == kind * 4 + p * 2 + mh, s, acc)
        full = jnp.concatenate([acc, jnp.zeros((LANES - half, LANES), F32)], axis=0)
        own[...] = jnp.transpose(full)[0:16]
        ca_src[0] = own[0:4]
        ca_src[1] = own[4:8]
        for k in range(1, ng):
            ca_copy(par, k).start()

    def communicate(n, par):
        for pc in range(2):
            for part in range(len(PARTS)):
                rows = pl.ds(*PARTS[part])
                rs_copy(pc, part, 0).wait_recv()
                rs_copy(pc, part, 1).wait_recv()
                at = near(-2)
                rho[pc, at, rows] = rho[pc, at, rows] + rsbuf[pc, 0, rows] + rsbuf[pc, 1, rows]
                rs_copy(pc, part, 5).start()
                rs_copy(pc, part, 2).wait_recv()
                at = near(2)
                rho[pc, at, rows] = rho[pc, at, rows] + rsbuf[pc, 2, rows]
                rs_copy(pc, part, 6).start()
            if pc == 0:
                send_direct(1)
        below = jnp.zeros((4, LANES), F32)
        above = jnp.zeros((4, LANES), F32)
        whole_in = ca_src[0]
        whole_out = ca_src[1]
        for k in range(1, ng):
            ca_copy(par, k).wait_recv()
            peer = lax.rem(g - k + ng, ng)
            got_in = ca_buf[par, k - 1, 0]
            got_out = ca_buf[par, k - 1, 1]
            below = below + got_in * jnp.where(peer < g, 1.0, 0.0).astype(F32)
            above = above + got_out * jnp.where(peer > g, 1.0, 0.0).astype(F32)
            whole_in = whole_in + got_in
            whole_out = whole_out + got_out
        cb_src[0] = whole_in
        cb_src[1] = whole_out
        for k in range(1, ny):
            cb_copy(par, k).start()

        @pl.when(r < nr - 1)
        def _():
            halo_copy(par, 0).start()

        @pl.when(r > 0)
        def _():
            halo_copy(par, 1).start()

        quarter = lax.rem(lax.div(z, 2), 2)
        for pc in range(2):
            tile = 2 * pc + lax.rem(z, 2)
            for part in range(len(PARTS)):
                size = PARTS[part][1]
                rows = pl.ds(*PARTS[part])
                for i in (3, 4, 5, 6):
                    rs_copy(pc, part, i).wait_recv()
                acc = (rho[pc, z, rows] + rsbuf[pc, 3, rows]) + (
                    rsbuf[pc, 4, rows] + rsbuf[pc, 5, rows]
                )
                acc = (acc + rsbuf[pc, 6, rows]) * delta
                up = up_t[tile, quarter, rows]
                dn = dn_t[tile, quarter, rows]

                def local(x, tri):
                    hi = x.astype(BF16).astype(F32)
                    both = jnp.concatenate([hi, x - hi], axis=0).astype(BF16)
                    s = dot(both, tri)
                    return s[:size] + s[size:]

                pot[pc, z, rows] = dn * local(acc * up, tri_in) + up * local(acc * dn, tri_out)
                for i in (0, 1):
                    ag_copy(pc, part, i).start()
            if pc == 0:
                for part in range(len(PARTS)):
                    for i in (2, 3):
                        ag_copy(pc, part, i).start()
        for k in range(1, ny):
            cb_copy(par, k).wait_recv()
            peer = lax.rem(y - k + ny, ny)
            below = below + cb_buf[par, k - 1, 0] * jnp.where(peer < y, 1.0, 0.0).astype(F32)
            above = above + cb_buf[par, k - 1, 1] * jnp.where(peer > y, 1.0, 0.0).astype(F32)
        cc_src[0] = below
        cc_src[1] = above + own[8:12]
        cc_src[2] = above
        for k in range(1, nz):
            cc_copy(par, k).start()

        @pl.when(r < nr - 1)
        def _():
            halo_copy(par, 0).wait_send()
            halo_copy(par, 1).wait_recv()

        @pl.when(r > 0)
        def _():
            halo_copy(par, 1).wait_send()
            halo_copy(par, 0).wait_recv()

        prepare(n, par, 0)
        for pc in range(2):
            for part in range(len(PARTS)):
                ag_copy(pc, part, 0).wait_recv()
                ag_copy(pc, part, 4).start()
                ag_copy(pc, part, 5).start()
                ag_copy(pc, part, 1).wait_recv()
                ag_copy(pc, part, 6).start()
            if pc == 0:
                for part in range(len(PARTS)):
                    for i in (2, 3):
                        ag_copy(1, part, i).start()
        prepare(n, par, 1)
        carry = [cc_src[kind] for kind in range(3)]
        for k in range(1, nz):
            cc_copy(par, k).wait_recv()
            carry = [carry[kind] + cc_buf[par, k - 1, kind] for kind in range(3)]
        for pc in range(2):
            for part in range(len(PARTS)):
                for i in range(7):
                    rs_copy(pc, part, i).wait_send()
        for k in range(1, ng):
            ca_copy(par, k).wait_send()
        for k in range(1, ny):
            cb_copy(par, k).wait_send()
        for k in range(1, nz):
            cc_copy(par, k).wait_send()

        for kind in range(3):
            own[4 * kind : 4 * kind + 4] = carry[kind]
        pad = jnp.zeros((LANES - 16, LANES), F32)
        return jnp.transpose(jnp.concatenate([own[...], pad], axis=0))[:half]

    def advance(n, par, pc, carry):
        base = pc * 2 * LANES
        for part in range(len(PARTS)):
            for i in (2, 3, 4, 5, 6):
                ag_copy(pc, part, i).wait_recv()
            for i in range(7):
                ag_copy(pc, part, i).wait_send()
        for p in range(2):
            cols = [[], []]
            for mh in range(2):
                k = 2 * p + mh
                t = 2 * pc
                first_pot = pot[pc, 4 * p + 2 * mh]
                second_pot = pot[pc, 4 * p + 2 * mh + 1]
                wide = (half, LANES)
                below = jnp.broadcast_to(carry[:, k : k + 1], wide)
                at = 4 * (pc + 1) + k
                above = jnp.broadcast_to(carry[:, at : at + 1], wide)
                in_first = jnp.broadcast_to(first_pot[:, LANES - 1 :], wide) * sc_in[t, mh]
                out_second = jnp.broadcast_to(second_pot[:, :1], wide) * sc_out[t + 1, mh]
                if pc == 0:
                    in_second = jnp.broadcast_to(second_pot[:, LANES - 1 :], wide)
                    tin01[k] = in_first + in_second * sc_in[t + 1, mh]
                else:
                    below = below + tin01[k]
                cols[0].append(
                    first_pot + dn_t[t, mh] * below + up_t[t, mh] * (above + out_second)
                )
                cols[1].append(
                    second_pot + dn_t[t + 1, mh] * (below + in_first) + up_t[t + 1, mh] * above
                )
            cols = [jnp.concatenate(parts, axis=0) for parts in cols]
            hi, lo = split2(jnp.concatenate(cols, axis=1))
            wide = dot(f_both[...], hi)
            field[pc, p] = wide[:chans] + (wide[chans:] + dot(f_both[:chans], lo))
        factor = jnp.where(n == 0, 2.0, 1.0).astype(F32)
        lanes = slice(base, base + 2 * LANES)
        for c0 in range(0, chans, ROWS_STEP):
            rows = slice(c0, c0 + ROWS_STEP)
            al = alpha[rows, lanes] * factor
            be = beta[rows, lanes] * factor
            ob = orb[rows, lanes]
            f0 = field[pc, 0, rows]
            f1 = field[pc, 1, rows]
            new = (
                known[0, rows, lanes] + (al * f1 - be * f0),
                known[1, rows, lanes] - (al * f0 + be * f1),
            )
            for p in range(2):
                vbuf[1 - par, p, rows, pl.ds(LANES + base, 2 * LANES)] = new[p]
                hi, lo = split2(new[p] * ob)
                w_hi[p, rows] = hi
                w_lo[p, rows] = lo

    spread_orbitals()
    load.wait()
    weigh(0, 0)
    densities(0)
    pl.semaphore_wait(barrier, 4 + (ng - 1) + (ny - 1))
    send_far(0)
    send_direct(0)
    weigh(0, 1)
    densities(1)
    send_far(1)
    power_tables()
    totals(0)
    diagonal_tables()

    def store(pc):
        at = pc * 2 * LANES
        return pltpu.make_async_copy(
            vbuf.at[SWEEPS % 2, :, :, pl.ds(LANES + at, 2 * LANES)],
            out_hbm.at[:, :, pl.ds(at, 2 * LANES)],
            io_sem.at[pc],
        )

    def sweep(n, c):
        par = lax.rem(n, 2)
        carry = communicate(n, par)
        for pc in range(2):
            advance(n, par, pc, carry)

            @pl.when(n < SWEEPS - 1)
            def _():
                densities(pc)
                send_far(pc)
                if pc == 0:
                    send_direct(0)

            @pl.when(n == SWEEPS - 1)
            def _():
                store(pc).start()

        @pl.when(n < SWEEPS - 1)
        def _():
            totals(1 - par)

        return c

    lax.fori_loop(0, SWEEPS, sweep, 0)
    for pc in range(2):
        store(pc).wait()


def body(nz, nr, wavefunc, orbitals, channel_orbital, channel_l, row_order, density, coupling):
    chans, width = wavefunc.shape[1:]
    rows = row_order.shape[0]
    half = rows // 2
    ng = 8 if nr % 8 == 0 else 2
    ny = nr // ng
    vmem = pl.BlockSpec(memory_space=pltpu.VMEM)
    hbm = pl.BlockSpec(memory_space=pl.ANY)
    dma = pltpu.SemaphoreType.DMA
    scratch = [
        pltpu.VMEM((2, 2, chans, width + 2 * LANES), F32),
        pltpu.VMEM((2, chans, width), F32),
        pltpu.VMEM((chans, width), F32),
        pltpu.VMEM((chans, width), F32),
        pltpu.VMEM((chans, width), F32),
        pltpu.VMEM((2, chans, width), F32),
        pltpu.VMEM((chans, width), F32),
        pltpu.VMEM((chans, width), F32),
        pltpu.VMEM((2, 2, chans, 2 * LANES), F32),
        pltpu.VMEM((2, chans, 2 * LANES), BF16),
        pltpu.VMEM((2, chans, 2 * LANES), BF16),
        pltpu.VMEM((4, 2, half, LANES), F32),
        pltpu.VMEM((4, 2, half, LANES), F32),
        pltpu.VMEM((2 * rows, chans), BF16),
        pltpu.VMEM((2 * chans, rows), BF16),
        pltpu.VMEM((2, 8, half, LANES), F32),
        pltpu.VMEM((2, 8, half, LANES), F32),
        pltpu.VMEM((2, 7, half, LANES), F32),
        pltpu.VMEM((16, LANES), F32),
        pltpu.VMEM((4, half, LANES), F32),
        pltpu.VMEM((4, 2, half, LANES), F32),
        pltpu.VMEM((4, 2, half, LANES), F32),
        pltpu.VMEM((2, 4, LANES), F32),
        pltpu.VMEM((2, ng - 1, 2, 4, LANES), F32),
        pltpu.VMEM((2, 4, LANES), F32),
        pltpu.VMEM((2, ny - 1, 2, 4, LANES), F32),
        pltpu.VMEM((3, 4, LANES), F32),
        pltpu.VMEM((2, nz - 1, 3, 4, LANES), F32),
        dma((2,)),
        dma((2, len(PARTS), 7)),
        dma((2, len(PARTS), 7)),
        dma((2, len(PARTS), 7)),
        dma((2, len(PARTS), 7)),
        dma((ng - 1,)),
        dma((2, ng - 1)),
        dma((ny - 1,)),
        dma((2, ny - 1)),
        dma((nz - 1,)),
        dma((2, nz - 1)),
        dma((2,)),
        dma((2, 2)),
    ]
    return pl.pallas_call(
        functools.partial(kernel, (nz, nr, ng, chans, width, half)),
        out_shape=jax.ShapeDtypeStruct(wavefunc.shape, F32),
        in_specs=[hbm] + [vmem] * 6,
        out_specs=hbm,
        scratch_shapes=scratch,
        compiler_params=pltpu.CompilerParams(
            collective_id=0, has_side_effects=True, vmem_limit_bytes=62 << 20
        ),
        name="cn_step",
    )(
        wavefunc,
        orbitals,
        channel_orbital.reshape(1, chans),
        channel_l.reshape(1, chans),
        row_order.reshape(1, rows),
        density,
        coupling.T,
    )


def solution(mesh):
    placed = (
        P(None, "chan", "rad"),
        P(None, "rad"),
        P("chan"),
        P("chan"),
        P(),
        P(None, "chan"),
        P("chan", None),
    )
    return jax.shard_map(
        functools.partial(body, mesh.shape["chan"], mesh.shape["rad"]),
        mesh=mesh,
        in_specs=placed,
        out_specs=P(None, "chan", "rad"),
        check_vma=False,
    )
```

```python
import functools

import jax
import jax.numpy as jnp
from jax import lax
from jax.experimental import pallas as pl
from jax.experimental.pallas import tpu as pltpu
from jax.sharding import PartitionSpec as P

SWEEPS = 4
MESH = pl.DeviceIdType.MESH
F32 = jnp.float32
BF16 = jnp.bfloat16
LANES = 128
SPAN = 400.0 / 408.0

RS_PLAN = ((-4, -2), (-3, -1), (3, 1), (-1, -1), (1, 1), (-2, -2), (2, 2))
AG_PLAN = ((0, 2), (0, -2), (0, 1), (0, -1), (-2, 2), (-2, 1), (2, -1))
PARTS = ((0, 40), (40, 32))
ROWS_STEP = 32


def split2(x):
    hi = x.astype(BF16)
    return hi, (x - hi.astype(F32)).astype(BF16)


def dot(a, b):
    return jnp.dot(a, b, preferred_element_type=F32)


def as_column(row):
    eight = jnp.broadcast_to(row, (8, row.shape[1]))
    first = lax.broadcasted_iota(jnp.int32, (8, LANES), 0) == 0
    return lax.dot_general(
        eight,
        jnp.where(first, 1.0, 0.0).astype(F32),
        (((0,), (0,)), ((), ())),
        precision=lax.Precision.HIGHEST,
        preferred_element_type=F32,
    )


def kernel(
    sizes,
    wave_hbm,
    orbitals_hbm,
    which_hbm,
    ell_hbm,
    order_hbm,
    density_hbm,
    coupling_hbm,
    out_hbm,
    orbitals_ref,
    which_ref,
    ell_ref,
    order_ref,
    density_ref,
    coupling_ref,
    vbuf,
    rhs,
    orb,
    diag,
    scl,
    known,
    alpha,
    beta,
    field,
    w_hi,
    w_lo,
    up_t,
    dn_t,
    d_both,
    f_both,
    rho,
    pot,
    rsbuf,
    own,
    tin01,
    sc_in,
    sc_out,
    ca_src,
    ca_buf,
    cb_src,
    cb_buf,
    cc_src,
    cc_buf,
    io_sem,
    rs_s,
    rs_r,
    ag_s,
    ag_r,
    ca_s,
    ca_r,
    cb_s,
    cb_r,
    cc_s,
    cc_r,
    ha_s,
    ha_r,
):
    nz, nr, ng, chans, width, half = sizes
    ny = nr // ng
    z = lax.axis_index("chan")
    r = lax.axis_index("rad")
    g = lax.rem(r, ng)
    y = lax.div(r, ng)
    total_rows = width * nr
    delta = SPAN / total_rows

    def zdev(offset):
        return (lax.rem(z + offset + nz, nz), r)

    sign = 1 - 2 * lax.rem(r, 2)

    def near(offset):
        return lax.rem(z + sign * offset + nz, nz)

    def gdev(k):
        return (z, y * ng + lax.rem(g + k, ng))

    def ydev(k):
        return (z, lax.rem(y + k, ny) * ng + g)

    barrier = pltpu.get_barrier_semaphore()

    def greet(device):
        pl.semaphore_signal(barrier, inc=1, device_id=device, device_id_type=MESH)

    for k in (1, 2, nz - 2, nz - 1):
        greet(zdev(k))
    for k in range(1, ng):
        greet(gdev(k))
    for k in range(1, ny):
        greet(ydev(k))
    greet((z, lax.rem(r + 1, nr)))
    greet((z, lax.rem(r + nr - 1, nr)))

    loads = [
        pltpu.make_async_copy(src, dst, io_sem.at[i])
        for i, (src, dst) in enumerate(
            (
                (which_hbm, which_ref),
                (orbitals_hbm, orbitals_ref),
                (wave_hbm, vbuf.at[0, :, :, pl.ds(LANES, width)]),
                (density_hbm, density_ref),
                (order_hbm, order_ref),
                (ell_hbm, ell_ref),
                (coupling_hbm, coupling_ref),
            )
        )
    ]
    for load in loads:
        load.start()

    @pl.when(r == 0)
    def _():
        for par in range(2):
            for p in range(2):
                vbuf[par, p, :, 0:LANES] = jnp.zeros((chans, LANES), F32)

    @pl.when(r == nr - 1)
    def _():
        for par in range(2):
            for p in range(2):
                vbuf[par, p, :, LANES + width :] = jnp.zeros((chans, LANES), F32)

    tiles = width // LANES
    i0 = lax.broadcasted_iota(jnp.int32, (LANES, LANES), 0)
    i1 = lax.broadcasted_iota(jnp.int32, (LANES, LANES), 1)
    tri_in = jnp.where(i0 <= i1, 1.0, 0.0).astype(BF16)
    tri_out = jnp.where(i0 > i1, 1.0, 0.0).astype(BF16)
    lane4 = lax.broadcasted_iota(jnp.int32, (4, LANES), 1)
    lane_id = lax.broadcasted_iota(jnp.int32, (half, LANES), 1)

    def spread_orbitals():
        which = as_column(which_ref[...].astype(F32))
        for t in range(tiles):
            lanes = slice(t * LANES, (t + 1) * LANES)
            for c0 in range(0, chans, ROWS_STEP):
                rows = slice(c0, c0 + ROWS_STEP)
                pick = which[rows]
                value = jnp.zeros((ROWS_STEP, LANES), F32)
                for o in range(orbitals_ref.shape[0]):
                    value = jnp.where(pick == float(o), orbitals_ref[o : o + 1, lanes], value)
                orb[rows, lanes] = value

    def split_density():
        hi, lo = split2(density_ref[...])
        d_both[: 2 * half] = hi
        d_both[2 * half :] = lo

    def radius_of(t):
        lane = lax.broadcasted_iota(jnp.int32, (1, LANES), 1)
        index = (r * width + t * LANES + lane).astype(F32)
        return 8.0 + 400.0 * (index + 0.5) / total_rows

    def power_tables():
        order = as_column(order_ref[...].astype(F32))
        for t in range(tiles):
            scaled = radius_of(t) / 408.0
            up = jnp.exp(order * jnp.log(scaled))
            dn = 1.0 / (up * scaled)
            inv_dn = jnp.broadcast_to((up * scaled)[:, LANES - 1 :], up.shape)
            inv_up = jnp.broadcast_to((dn * scaled)[:, :1], up.shape)
            for mh in range(2):
                rows = slice(mh * half, (mh + 1) * half)
                up_t[t, mh] = up[rows]
                dn_t[t, mh] = dn[rows]
                sc_in[t, mh] = inv_dn[rows]
                sc_out[t, mh] = inv_up[rows]

    def diagonal_tables():
        ell = as_column(ell_ref[...].astype(F32))
        strength = ell * (ell + 1.0)
        for t in range(tiles):
            radius = radius_of(t)
            inv = 1.0 / (4.0 * radius * radius)
            lanes = slice(t * LANES, (t + 1) * LANES)
            for c0 in range(0, chans, ROWS_STEP):
                rows = slice(c0, c0 + ROWS_STEP)
                dg = 0.5 + strength[rows] * inv
                sc = 1.0 / (1.0 + dg * dg)
                al = sc * orb[rows, lanes]
                diag[rows, lanes] = dg
                scl[rows, lanes] = sc
                alpha[rows, lanes] = al
                beta[rows, lanes] = al * dg
        turned = jnp.concatenate(
            [coupling_ref[...], jnp.zeros((chans - 2 * half, chans), F32)], axis=0
        )
        hi, lo = split2(jnp.transpose(turned)[:, : 2 * half])
        f_both[:chans] = hi
        f_both[chans:] = lo

    def rs_copy(pc, part, i):
        chunk, target = RS_PLAN[i]
        rows = pl.ds(*PARTS[part])
        return pltpu.make_async_remote_copy(
            src_ref=rho.at[pc, near(chunk), rows],
            dst_ref=rsbuf.at[pc, i, rows],
            send_sem=rs_s.at[pc, part, i],
            recv_sem=rs_r.at[pc, part, i],
            device_id=(near(target), r),
            device_id_type=MESH,
        )

    def ag_copy(pc, part, i):
        chunk, target = AG_PLAN[i]
        place = pot.at[pc, near(chunk), pl.ds(*PARTS[part])]
        return pltpu.make_async_remote_copy(
            src_ref=place,
            dst_ref=place,
            send_sem=ag_s.at[pc, part, i],
            recv_sem=ag_r.at[pc, part, i],
            device_id=(near(target), r),
            device_id_type=MESH,
        )

    def small_copy(src, buf, send, recv, par, k, device):
        return pltpu.make_async_remote_copy(
            src_ref=src,
            dst_ref=buf.at[par, k - 1],
            send_sem=send.at[k - 1],
            recv_sem=recv.at[par, k - 1],
            device_id=device,
            device_id_type=MESH,
        )

    def ca_copy(par, k):
        return small_copy(ca_src, ca_buf, ca_s, ca_r, par, k, gdev(k))

    def cb_copy(par, k):
        return small_copy(cb_src, cb_buf, cb_s, cb_r, par, k, ydev(k))

    def cc_copy(par, k):
        return small_copy(cc_src, cc_buf, cc_s, cc_r, par, k, zdev(k))

    def halo_copy(par, side):
        here, there = (width, 0) if side == 0 else (LANES, LANES + width)
        to = r + 1 if side == 0 else r - 1
        to = lax.rem(to + nr, nr)
        return pltpu.make_async_remote_copy(
            src_ref=vbuf.at[par, :, :, pl.ds(here, LANES)],
            dst_ref=vbuf.at[par, :, :, pl.ds(there, LANES)],
            send_sem=ha_s.at[side],
            recv_sem=ha_r.at[par, side],
            device_id=(z, to),
            device_id_type=MESH,
        )

    def weigh(par, pc):
        lanes = slice(pc * 2 * LANES, (pc + 1) * 2 * LANES)
        for c0 in range(0, chans, ROWS_STEP):
            rows = slice(c0, c0 + ROWS_STEP)
            for p in range(2):
                v = vbuf[par, p, rows, LANES + lanes.start : LANES + lanes.stop]
                hi, lo = split2(v * orb[rows, lanes])
                w_hi[p, rows] = hi
                w_lo[p, rows] = lo

    def densities(pc):
        rows = 2 * half
        for p in range(2):
            wide = dot(d_both[...], w_hi[p])
            part = wide[:rows] + (wide[rows:] + dot(d_both[:rows], w_lo[p]))
            for mh in range(2):
                for h in range(2):
                    rho[pc, 4 * p + 2 * mh + h] = part[
                        mh * half : (mh + 1) * half, h * LANES : (h + 1) * LANES
                    ]

    def prepare(n, par, pc):
        base = pc * 2 * LANES
        lanes = slice(base, base + 2 * LANES)

        def kinetic(rows):
            v, kin = [], []
            for p in range(2):
                x = vbuf[par, p, rows, pl.ds(base, 4 * LANES)]
                left = pltpu.roll(x, 1, 1)[:, LANES : 3 * LANES]
                right = pltpu.roll(x, 4 * LANES - 1, 1)[:, LANES : 3 * LANES]
                v.append(x[:, LANES : 3 * LANES])
                kin.append(-0.25 * (left + right))
            return v, kin

        @pl.when(n == 0)
        def _():
            for c0 in range(0, chans, ROWS_STEP):
                rows = slice(c0, c0 + ROWS_STEP)
                v, kin = kinetic(rows)
                dg = diag[rows, lanes]
                rhs[0, rows, lanes] = v[0] + (kin[1] + dg * v[1])
                rhs[1, rows, lanes] = v[1] - (kin[0] + dg * v[0])

        @pl.when(n == 1)
        def _():
            for c0 in range(0, chans, ROWS_STEP):
                rows = slice(c0, c0 + ROWS_STEP)
                ob = orb[rows, lanes]
                rhs[0, rows, lanes] = rhs[0, rows, lanes] + field[pc, 1, rows] * ob
                rhs[1, rows, lanes] = rhs[1, rows, lanes] - field[pc, 0, rows] * ob

        for c0 in range(0, chans, ROWS_STEP):
            rows = slice(c0, c0 + ROWS_STEP)
            v, kin = kinetic(rows)
            dg = diag[rows, lanes]
            sc = scl[rows, lanes]
            q0 = rhs[0, rows, lanes] + kin[1]
            q1 = rhs[1, rows, lanes] - kin[0]
            known[0, rows, lanes] = (q0 + dg * q1) * sc
            known[1, rows, lanes] = (q1 - dg * q0) * sc

    def send_far(pc):
        for part in range(len(PARTS)):
            for i in (0, 1, 2):
                rs_copy(pc, part, i).start()

    def send_direct(pc):
        for part in range(len(PARTS)):
            for i in (3, 4):
                rs_copy(pc, part, i).start()

    def totals():
        acc = jnp.zeros((half, LANES), F32)
        for p in range(2):
            for mh in range(2):
                blocks = [rho[t // 2, 4 * p + 2 * mh + t % 2] * delta for t in range(tiles)]
                ups = [blocks[t] * up_t[t, mh] for t in range(tiles)]
                dns = [blocks[t] * dn_t[t, mh] for t in range(tiles)]
                near_out = dns[0] + dns[1]
                far_out = dns[2] + dns[3]
                sums = ((ups[0] + ups[1]) + (ups[2] + ups[3]), near_out + far_out, far_out)
                for kind in range(3):
                    s = jnp.sum(sums[kind], axis=1, keepdims=True)
                    acc = jnp.where(lane_id == kind * 4 + p * 2 + mh, s, acc)
        full = jnp.concatenate([acc, jnp.zeros((LANES - half, LANES), F32)], axis=0)
        own[...] = jnp.transpose(full)[0:16]
        ca_src[0] = own[0:4]
        ca_src[1] = own[4:8]

    def send_totals(par):
        for k in range(1, ng):
            ca_copy(par, k).start()

        @pl.when(r < nr - 1)
        def _():
            halo_copy(par, 0).start()

        @pl.when(r > 0)
        def _():
            halo_copy(par, 1).start()

    def communicate(n, par):
        for pc in range(2):
            for part in range(len(PARTS)):
                rows = pl.ds(*PARTS[part])
                rs_copy(pc, part, 0).wait_recv()
                rs_copy(pc, part, 1).wait_recv()
                at = near(-2)
                rho[pc, at, rows] = rho[pc, at, rows] + rsbuf[pc, 0, rows] + rsbuf[pc, 1, rows]
                rs_copy(pc, part, 5).start()
                rs_copy(pc, part, 2).wait_recv()
                at = near(2)
                rho[pc, at, rows] = rho[pc, at, rows] + rsbuf[pc, 2, rows]
                rs_copy(pc, part, 6).start()
            if pc == 0:
                send_direct(1)
        below = jnp.zeros((4, LANES), F32)
        above = jnp.zeros((4, LANES), F32)
        whole_in = ca_src[0]
        whole_out = ca_src[1]
        for k in range(1, ng):
            ca_copy(par, k).wait_recv()
            peer = lax.rem(g - k + ng, ng)
            got_in = ca_buf[par, k - 1, 0]
            got_out = ca_buf[par, k - 1, 1]
            below = below + got_in * jnp.where(peer < g, 1.0, 0.0).astype(F32)
            above = above + got_out * jnp.where(peer > g, 1.0, 0.0).astype(F32)
            whole_in = whole_in + got_in
            whole_out = whole_out + got_out
        cb_src[0] = whole_in
        cb_src[1] = whole_out
        for k in range(1, ny):
            cb_copy(par, k).start()

        quarter = lax.rem(lax.div(z, 2), 2)
        for pc in range(2):
            tile = 2 * pc + lax.rem(z, 2)
            for part in range(len(PARTS)):
                size = PARTS[part][1]
                rows = pl.ds(*PARTS[part])
                for i in (3, 4, 5, 6):
                    rs_copy(pc, part, i).wait_recv()
                acc = (rho[pc, z, rows] + rsbuf[pc, 3, rows]) + (
                    rsbuf[pc, 4, rows] + rsbuf[pc, 5, rows]
                )
                acc = (acc + rsbuf[pc, 6, rows]) * delta
                up = up_t[tile, quarter, rows]
                dn = dn_t[tile, quarter, rows]

                def local(x, tri):
                    hi = x.astype(BF16).astype(F32)
                    both = jnp.concatenate([hi, x - hi], axis=0).astype(BF16)
                    s = dot(both, tri)
                    return s[:size] + s[size:]

                pot[pc, z, rows] = dn * local(acc * up, tri_in) + up * local(acc * dn, tri_out)
                for i in (0, 1):
                    ag_copy(pc, part, i).start()
            if pc == 0:
                for part in range(len(PARTS)):
                    for i in (2, 3):
                        ag_copy(pc, part, i).start()
        for k in range(1, ny):
            cb_copy(par, k).wait_recv()
            peer = lax.rem(y - k + ny, ny)
            below = below + cb_buf[par, k - 1, 0] * jnp.where(peer < y, 1.0, 0.0).astype(F32)
            above = above + cb_buf[par, k - 1, 1] * jnp.where(peer > y, 1.0, 0.0).astype(F32)
        far = own[8:12]
        cc_src[0] = jnp.where(lane4 < half, below, pltpu.roll(far, half, 1))
        cc_src[1] = jnp.where(lane4 < half, above, pltpu.roll(far, 2 * half - LANES, 1))
        for k in range(1, nz):
            cc_copy(par, k).start()

        @pl.when(r < nr - 1)
        def _():
            halo_copy(par, 0).wait_send()
            halo_copy(par, 1).wait_recv()

        @pl.when(r > 0)
        def _():
            halo_copy(par, 1).wait_send()
            halo_copy(par, 0).wait_recv()

        prepare(n, par, 0)
        for pc in range(2):
            for part in range(len(PARTS)):
                ag_copy(pc, part, 0).wait_recv()
                ag_copy(pc, part, 4).start()
                ag_copy(pc, part, 5).start()
                ag_copy(pc, part, 1).wait_recv()
                ag_copy(pc, part, 6).start()
            if pc == 0:
                for part in range(len(PARTS)):
                    for i in (2, 3):
                        ag_copy(1, part, i).start()
        prepare(n, par, 1)
        carry = [cc_src[kind] for kind in range(2)]
        for k in range(1, nz):
            cc_copy(par, k).wait_recv()
            carry = [carry[kind] + cc_buf[par, k - 1, kind] for kind in range(2)]
        for pc in range(2):
            for part in range(len(PARTS)):
                for i in range(7):
                    rs_copy(pc, part, i).wait_send()
        for k in range(1, ng):
            ca_copy(par, k).wait_send()
        for k in range(1, ny):
            cb_copy(par, k).wait_send()
        for k in range(1, nz):
            cc_copy(par, k).wait_send()

        first = pltpu.roll(carry[0], LANES - half, 1)
        second = pltpu.roll(carry[1], 2 * LANES - 2 * half, 1)
        far = jnp.where(lane4 < LANES - half, first, second)
        own[0:4] = carry[0]
        own[4:8] = carry[1] + far
        own[8:12] = carry[1]
        pad = jnp.zeros((LANES - 16, LANES), F32)
        return jnp.transpose(jnp.concatenate([own[...], pad], axis=0))[:half]

    def advance(n, par, pc, carry):
        base = pc * 2 * LANES
        for part in range(len(PARTS)):
            for i in (2, 3, 4, 5, 6):
                ag_copy(pc, part, i).wait_recv()
        for p in range(2):
            cols = [[], []]
            for mh in range(2):
                k = 2 * p + mh
                t = 2 * pc
                first_pot = pot[pc, 4 * p + 2 * mh]
                second_pot = pot[pc, 4 * p + 2 * mh + 1]
                wide = (half, LANES)
                below = jnp.broadcast_to(carry[:, k : k + 1], wide)
                at = 4 * (pc + 1) + k
                above = jnp.broadcast_to(carry[:, at : at + 1], wide)
                in_first = jnp.broadcast_to(first_pot[:, LANES - 1 :], wide) * sc_in[t, mh]
                out_second = jnp.broadcast_to(second_pot[:, :1], wide) * sc_out[t + 1, mh]
                if pc == 0:
                    in_second = jnp.broadcast_to(second_pot[:, LANES - 1 :], wide)
                    tin01[k] = in_first + in_second * sc_in[t + 1, mh]
                else:
                    below = below + tin01[k]
                cols[0].append(
                    first_pot + dn_t[t, mh] * below + up_t[t, mh] * (above + out_second)
                )
                cols[1].append(
                    second_pot + dn_t[t + 1, mh] * (below + in_first) + up_t[t + 1, mh] * above
                )
            cols = [jnp.concatenate(parts, axis=0) for parts in cols]
            hi, lo = split2(jnp.concatenate(cols, axis=1))
            wide = dot(f_both[...], hi)
            field[pc, p] = wide[:chans] + (wide[chans:] + dot(f_both[:chans], lo))
        factor = jnp.where(n == 0, 2.0, 1.0).astype(F32)
        lanes = slice(base, base + 2 * LANES)
        for c0 in range(0, chans, ROWS_STEP):
            rows = slice(c0, c0 + ROWS_STEP)
            al = alpha[rows, lanes] * factor
            be = beta[rows, lanes] * factor
            ob = orb[rows, lanes]
            f0 = field[pc, 0, rows]
            f1 = field[pc, 1, rows]
            new = (
                known[0, rows, lanes] + (al * f1 - be * f0),
                known[1, rows, lanes] - (al * f0 + be * f1),
            )
            for p in range(2):
                vbuf[1 - par, p, rows, pl.ds(LANES + base, 2 * LANES)] = new[p]
                hi, lo = split2(new[p] * ob)
                w_hi[p, rows] = hi
                w_lo[p, rows] = lo

    loads[0].wait()
    loads[1].wait()
    spread_orbitals()
    loads[2].wait()
    weigh(0, 0)
    loads[3].wait()
    split_density()
    densities(0)
    pl.semaphore_wait(barrier, 4 + (ng - 1) + (ny - 1) + 2)
    send_far(0)
    send_direct(0)
    weigh(0, 1)
    densities(1)
    send_far(1)
    loads[4].wait()
    power_tables()
    totals()
    send_totals(0)
    loads[5].wait()
    loads[6].wait()
    diagonal_tables()

    def store(pc):
        at = pc * 2 * LANES
        return pltpu.make_async_copy(
            vbuf.at[SWEEPS % 2, :, :, pl.ds(LANES + at, 2 * LANES)],
            out_hbm.at[:, :, pl.ds(at, 2 * LANES)],
            io_sem.at[pc],
        )

    def sweep(n, c):
        par = lax.rem(n, 2)
        carry = communicate(n, par)
        for pc in range(2):
            advance(n, par, pc, carry)

            @pl.when(n < SWEEPS - 1)
            def _():
                densities(pc)

            for part in range(len(PARTS)):
                for i in range(7):
                    ag_copy(pc, part, i).wait_send()

            @pl.when(n < SWEEPS - 1)
            def _():
                send_far(pc)
                if pc == 0:
                    send_direct(0)

            @pl.when(n == SWEEPS - 1)
            def _():
                store(pc).start()

        @pl.when(n < SWEEPS - 1)
        def _():
            totals()
            send_totals(1 - par)

        return c

    lax.fori_loop(0, SWEEPS, sweep, 0)
    for pc in range(2):
        store(pc).wait()


def body(nz, nr, wavefunc, orbitals, channel_orbital, channel_l, row_order, density, coupling):
    chans, width = wavefunc.shape[1:]
    rows = row_order.shape[0]
    half = rows // 2
    ng = 8 if nr % 8 == 0 else 2
    ny = nr // ng
    hbm = pl.BlockSpec(memory_space=pl.ANY)
    dma = pltpu.SemaphoreType.DMA
    scratch = [
        pltpu.VMEM(orbitals.shape, F32),
        pltpu.VMEM((1, chans), jnp.int32),
        pltpu.VMEM((1, chans), jnp.int32),
        pltpu.VMEM((1, rows), jnp.int32),
        pltpu.VMEM((rows, chans), F32),
        pltpu.VMEM((rows, chans), F32),
        pltpu.VMEM((2, 2, chans, width + 2 * LANES), F32),
        pltpu.VMEM((2, chans, width), F32),
        pltpu.VMEM((chans, width), F32),
        pltpu.VMEM((chans, width), F32),
        pltpu.VMEM((chans, width), F32),
        pltpu.VMEM((2, chans, width), F32),
        pltpu.VMEM((chans, width), F32),
        pltpu.VMEM((chans, width), F32),
        pltpu.VMEM((2, 2, chans, 2 * LANES), F32),
        pltpu.VMEM((2, chans, 2 * LANES), BF16),
        pltpu.VMEM((2, chans, 2 * LANES), BF16),
        pltpu.VMEM((4, 2, half, LANES), F32),
        pltpu.VMEM((4, 2, half, LANES), F32),
        pltpu.VMEM((2 * rows, chans), BF16),
        pltpu.VMEM((2 * chans, rows), BF16),
        pltpu.VMEM((2, 8, half, LANES), F32),
        pltpu.VMEM((2, 8, half, LANES), F32),
        pltpu.VMEM((2, 7, half, LANES), F32),
        pltpu.VMEM((16, LANES), F32),
        pltpu.VMEM((4, half, LANES), F32),
        pltpu.VMEM((4, 2, half, LANES), F32),
        pltpu.VMEM((4, 2, half, LANES), F32),
        pltpu.VMEM((2, 4, LANES), F32),
        pltpu.VMEM((2, ng - 1, 2, 4, LANES), F32),
        pltpu.VMEM((2, 4, LANES), F32),
        pltpu.VMEM((2, ny - 1, 2, 4, LANES), F32),
        pltpu.VMEM((2, 4, LANES), F32),
        pltpu.VMEM((2, nz - 1, 2, 4, LANES), F32),
        dma((7,)),
        dma((2, len(PARTS), 7)),
        dma((2, len(PARTS), 7)),
        dma((2, len(PARTS), 7)),
        dma((2, len(PARTS), 7)),
        dma((ng - 1,)),
        dma((2, ng - 1)),
        dma((ny - 1,)),
        dma((2, ny - 1)),
        dma((nz - 1,)),
        dma((2, nz - 1)),
        dma((2,)),
        dma((2, 2)),
    ]
    return pl.pallas_call(
        functools.partial(kernel, (nz, nr, ng, chans, width, half)),
        out_shape=jax.ShapeDtypeStruct(wavefunc.shape, F32),
        in_specs=[hbm] * 7,
        out_specs=hbm,
        scratch_shapes=scratch,
        compiler_params=pltpu.CompilerParams(
            collective_id=0, has_side_effects=True, vmem_limit_bytes=62 << 20
        ),
        name="cn_step",
    )(
        wavefunc,
        orbitals,
        channel_orbital.reshape(1, chans),
        channel_l.reshape(1, chans),
        row_order.reshape(1, rows),
        density,
        coupling.T,
    )


def solution(mesh):
    placed = (
        P(None, "chan", "rad"),
        P(None, "rad"),
        P("chan"),
        P("chan"),
        P(),
        P(None, "chan"),
        P("chan", None),
    )
    return jax.shard_map(
        functools.partial(body, mesh.shape["chan"], mesh.shape["rad"]),
        mesh=mesh,
        in_specs=placed,
        out_specs=P(None, "chan", "rad"),
        check_vma=False,
    )
```

```python
import functools

import jax
import jax.numpy as jnp
from jax import lax
from jax.experimental import pallas as pl
from jax.experimental.pallas import tpu as pltpu
from jax.sharding import PartitionSpec as P

SWEEPS = 4
MESH = pl.DeviceIdType.MESH
F32 = jnp.float32
BF16 = jnp.bfloat16
LANES = 128
SPAN = 400.0 / 408.0

RS_PLAN = ((-4, -2), (-3, -1), (3, 1), (-1, -1), (1, 1), (-2, -2), (2, 2))
AG_PLAN = ((0, 2), (0, -2), (0, 1), (0, -1), (-2, 2), (-2, 1), (2, -1))
PARTS = ((0, 40), (40, 32))
ROWS_STEP = 32


def split2(x):
    hi = x.astype(BF16)
    return hi, (x - hi.astype(F32)).astype(BF16)


def dot(a, b):
    return jnp.dot(a, b, preferred_element_type=F32)


def as_column(row):
    eight = jnp.broadcast_to(row, (8, row.shape[1]))
    first = lax.broadcasted_iota(jnp.int32, (8, LANES), 0) == 0
    return lax.dot_general(
        eight,
        jnp.where(first, 1.0, 0.0).astype(F32),
        (((0,), (0,)), ((), ())),
        precision=lax.Precision.HIGHEST,
        preferred_element_type=F32,
    )


def kernel(
    sizes,
    wave_hbm,
    orbitals_hbm,
    which_hbm,
    ell_hbm,
    order_hbm,
    density_hbm,
    coupling_hbm,
    out_hbm,
    orbitals_ref,
    which_ref,
    ell_ref,
    order_ref,
    density_ref,
    coupling_ref,
    vbuf,
    rhs,
    orb,
    diag,
    scl,
    known,
    alpha,
    beta,
    field,
    w_hi,
    w_lo,
    up_t,
    dn_t,
    d_both,
    f_both,
    rho,
    pot,
    rsbuf,
    own,
    tin01,
    sc_in,
    sc_out,
    ca_src,
    ca_buf,
    cb_src,
    cb_buf,
    cc_src,
    cc_buf,
    io_sem,
    rs_s,
    rs_r,
    ag_s,
    ag_r,
    ca_s,
    ca_r,
    cb_s,
    cb_r,
    cc_s,
    cc_r,
    ha_s,
    ha_r,
):
    nz, nr, ng, chans, width, half = sizes
    ny = nr // ng
    z = lax.axis_index("chan")
    r = lax.axis_index("rad")
    g = lax.rem(r, ng)
    y = lax.div(r, ng)
    total_rows = width * nr
    delta = SPAN / total_rows

    def zdev(offset):
        return (lax.rem(z + offset + nz, nz), r)

    sign = 1 - 2 * lax.rem(r, 2)

    def near(offset):
        return lax.rem(z + sign * offset + nz, nz)

    def gdev(k):
        return (z, y * ng + lax.rem(g + k, ng))

    def ydev(k):
        return (z, lax.rem(y + k, ny) * ng + g)

    barrier = pltpu.get_barrier_semaphore()

    def greet(device):
        pl.semaphore_signal(barrier, inc=1, device_id=device, device_id_type=MESH)

    for k in (1, 2, nz - 2, nz - 1):
        greet(zdev(k))
    for k in range(1, ng):
        greet(gdev(k))
    for k in range(1, ny):
        greet(ydev(k))
    greet((z, lax.rem(r + 1, nr)))
    greet((z, lax.rem(r + nr - 1, nr)))

    loads = [
        pltpu.make_async_copy(src, dst, io_sem.at[i])
        for i, (src, dst) in enumerate(
            (
                (which_hbm, which_ref),
                (orbitals_hbm, orbitals_ref),
                (wave_hbm, vbuf.at[0, :, :, pl.ds(LANES, width)]),
                (density_hbm, density_ref),
                (order_hbm, order_ref),
                (ell_hbm, ell_ref),
                (coupling_hbm, coupling_ref),
            )
        )
    ]
    for load in loads:
        load.start()

    @pl.when(r == 0)
    def _():
        for par in range(2):
            for p in range(2):
                vbuf[par, p, :, 0:LANES] = jnp.zeros((chans, LANES), F32)

    @pl.when(r == nr - 1)
    def _():
        for par in range(2):
            for p in range(2):
                vbuf[par, p, :, LANES + width :] = jnp.zeros((chans, LANES), F32)

    tiles = width // LANES
    i0 = lax.broadcasted_iota(jnp.int32, (2 * LANES, 2 * LANES), 0)
    i1 = lax.broadcasted_iota(jnp.int32, (2 * LANES, 2 * LANES), 1)
    inner = (i0 < LANES) & (i1 < LANES) & (i0 <= i1)
    outer = (i0 >= LANES) & (i1 >= LANES) & (i0 > i1)
    tri = jnp.where(inner | outer, 1.0, 0.0).astype(BF16)
    lane4 = lax.broadcasted_iota(jnp.int32, (4, LANES), 1)
    lane_id = lax.broadcasted_iota(jnp.int32, (half, LANES), 1)

    def spread_orbitals():
        which = as_column(which_ref[...].astype(F32))
        for t in range(tiles):
            lanes = slice(t * LANES, (t + 1) * LANES)
            for c0 in range(0, chans, ROWS_STEP):
                rows = slice(c0, c0 + ROWS_STEP)
                pick = which[rows]
                value = jnp.zeros((ROWS_STEP, LANES), F32)
                for o in range(orbitals_ref.shape[0]):
                    value = jnp.where(pick == float(o), orbitals_ref[o : o + 1, lanes], value)
                orb[rows, lanes] = value

    def split_density():
        hi, lo = split2(density_ref[...])
        d_both[: 2 * half] = hi
        d_both[2 * half :] = lo

    def radius_of(t):
        lane = lax.broadcasted_iota(jnp.int32, (1, LANES), 1)
        index = (r * width + t * LANES + lane).astype(F32)
        return 8.0 + 400.0 * (index + 0.5) / total_rows

    def power_tables():
        order = as_column(order_ref[...].astype(F32))
        for t in range(tiles):
            scaled = radius_of(t) / 408.0
            up = jnp.exp(order * jnp.log(scaled))
            dn = 1.0 / (up * scaled)
            inv_dn = jnp.broadcast_to((up * scaled)[:, LANES - 1 :], up.shape)
            inv_up = jnp.broadcast_to((dn * scaled)[:, :1], up.shape)
            for mh in range(2):
                rows = slice(mh * half, (mh + 1) * half)
                up_t[t, mh] = up[rows]
                dn_t[t, mh] = dn[rows]
                sc_in[t, mh] = inv_dn[rows]
                sc_out[t, mh] = inv_up[rows]

    def diagonal_tables():
        ell = as_column(ell_ref[...].astype(F32))
        strength = ell * (ell + 1.0)
        for t in range(tiles):
            radius = radius_of(t)
            inv = 1.0 / (4.0 * radius * radius)
            lanes = slice(t * LANES, (t + 1) * LANES)
            for c0 in range(0, chans, ROWS_STEP):
                rows = slice(c0, c0 + ROWS_STEP)
                dg = 0.5 + strength[rows] * inv
                sc = 1.0 / (1.0 + dg * dg)
                al = sc * orb[rows, lanes]
                diag[rows, lanes] = dg
                scl[rows, lanes] = sc
                alpha[rows, lanes] = al
                beta[rows, lanes] = al * dg
        turned = jnp.concatenate(
            [coupling_ref[...], jnp.zeros((chans - 2 * half, chans), F32)], axis=0
        )
        hi, lo = split2(jnp.transpose(turned)[:, : 2 * half])
        f_both[:chans] = hi
        f_both[chans:] = lo

    def rs_copy(pc, part, i):
        chunk, target = RS_PLAN[i]
        rows = pl.ds(*PARTS[part])
        return pltpu.make_async_remote_copy(
            src_ref=rho.at[pc, near(chunk), rows],
            dst_ref=rsbuf.at[pc, i, rows],
            send_sem=rs_s.at[pc, part, i],
            recv_sem=rs_r.at[pc, part, i],
            device_id=(near(target), r),
            device_id_type=MESH,
        )

    def ag_copy(pc, part, i):
        chunk, target = AG_PLAN[i]
        place = pot.at[pc, near(chunk), pl.ds(*PARTS[part])]
        return pltpu.make_async_remote_copy(
            src_ref=place,
            dst_ref=place,
            send_sem=ag_s.at[pc, part, i],
            recv_sem=ag_r.at[pc, part, i],
            device_id=(near(target), r),
            device_id_type=MESH,
        )

    def small_copy(src, buf, send, recv, par, k, device):
        return pltpu.make_async_remote_copy(
            src_ref=src,
            dst_ref=buf.at[par, k - 1],
            send_sem=send.at[k - 1],
            recv_sem=recv.at[par, k - 1],
            device_id=device,
            device_id_type=MESH,
        )

    def ca_copy(par, k):
        return small_copy(ca_src, ca_buf, ca_s, ca_r, par, k, gdev(k))

    def cb_copy(par, k):
        return small_copy(cb_src, cb_buf, cb_s, cb_r, par, k, ydev(k))

    def cc_copy(par, k):
        return small_copy(cc_src, cc_buf, cc_s, cc_r, par, k, zdev(k))

    def halo_copy(par, side):
        here, there = (width, 0) if side == 0 else (LANES, LANES + width)
        to = r + 1 if side == 0 else r - 1
        to = lax.rem(to + nr, nr)
        return pltpu.make_async_remote_copy(
            src_ref=vbuf.at[par, :, :, pl.ds(here, LANES)],
            dst_ref=vbuf.at[par, :, :, pl.ds(there, LANES)],
            send_sem=ha_s.at[side],
            recv_sem=ha_r.at[par, side],
            device_id=(z, to),
            device_id_type=MESH,
        )

    def weigh(par, pc):
        lanes = slice(pc * 2 * LANES, (pc + 1) * 2 * LANES)
        for c0 in range(0, chans, ROWS_STEP):
            rows = slice(c0, c0 + ROWS_STEP)
            for p in range(2):
                v = vbuf[par, p, rows, LANES + lanes.start : LANES + lanes.stop]
                hi, lo = split2(v * orb[rows, lanes])
                w_hi[p, rows] = hi
                w_lo[p, rows] = lo

    def densities(pc):
        rows = 2 * half
        for p in range(2):
            wide = dot(d_both[...], w_hi[p])
            part = wide[:rows] + (wide[rows:] + dot(d_both[:rows], w_lo[p]))
            for mh in range(2):
                for h in range(2):
                    rho[pc, 4 * p + 2 * mh + h] = part[
                        mh * half : (mh + 1) * half, h * LANES : (h + 1) * LANES
                    ]

    def prepare(n, par, pc):
        base = pc * 2 * LANES
        lanes = slice(base, base + 2 * LANES)

        def kinetic(rows):
            v, kin = [], []
            for p in range(2):
                x = vbuf[par, p, rows, pl.ds(base, 4 * LANES)]
                left = pltpu.roll(x, 1, 1)[:, LANES : 3 * LANES]
                right = pltpu.roll(x, 4 * LANES - 1, 1)[:, LANES : 3 * LANES]
                v.append(x[:, LANES : 3 * LANES])
                kin.append(-0.25 * (left + right))
            return v, kin

        @pl.when(n == 0)
        def _():
            for c0 in range(0, chans, ROWS_STEP):
                rows = slice(c0, c0 + ROWS_STEP)
                v, kin = kinetic(rows)
                dg = diag[rows, lanes]
                rhs[0, rows, lanes] = v[0] + (kin[1] + dg * v[1])
                rhs[1, rows, lanes] = v[1] - (kin[0] + dg * v[0])

        @pl.when(n == 1)
        def _():
            for c0 in range(0, chans, ROWS_STEP):
                rows = slice(c0, c0 + ROWS_STEP)
                ob = orb[rows, lanes]
                rhs[0, rows, lanes] = rhs[0, rows, lanes] + field[pc, 1, rows] * ob
                rhs[1, rows, lanes] = rhs[1, rows, lanes] - field[pc, 0, rows] * ob

        for c0 in range(0, chans, ROWS_STEP):
            rows = slice(c0, c0 + ROWS_STEP)
            v, kin = kinetic(rows)
            dg = diag[rows, lanes]
            sc = scl[rows, lanes]
            q0 = rhs[0, rows, lanes] + kin[1]
            q1 = rhs[1, rows, lanes] - kin[0]
            known[0, rows, lanes] = (q0 + dg * q1) * sc
            known[1, rows, lanes] = (q1 - dg * q0) * sc

    def send_far(pc):
        for part in range(len(PARTS)):
            for i in (0, 1, 2):
                rs_copy(pc, part, i).start()

    def send_direct(pc):
        for part in range(len(PARTS)):
            for i in (3, 4):
                rs_copy(pc, part, i).start()

    def totals():
        acc = jnp.zeros((half, LANES), F32)
        for p in range(2):
            for mh in range(2):
                blocks = [rho[t // 2, 4 * p + 2 * mh + t % 2] * delta for t in range(tiles)]
                ups = [blocks[t] * up_t[t, mh] for t in range(tiles)]
                dns = [blocks[t] * dn_t[t, mh] for t in range(tiles)]
                near_out = dns[0] + dns[1]
                far_out = dns[2] + dns[3]
                sums = ((ups[0] + ups[1]) + (ups[2] + ups[3]), near_out + far_out, far_out)
                for kind in range(3):
                    s = jnp.sum(sums[kind], axis=1, keepdims=True)
                    acc = jnp.where(lane_id == kind * 4 + p * 2 + mh, s, acc)
        full = jnp.concatenate([acc, jnp.zeros((LANES - half, LANES), F32)], axis=0)
        own[...] = jnp.transpose(full)[0:16]
        ca_src[0] = own[0:4]
        ca_src[1] = own[4:8]

    def send_totals(par):
        for k in range(1, ng):
            ca_copy(par, k).start()

        @pl.when(r < nr - 1)
        def _():
            halo_copy(par, 0).start()

        @pl.when(r > 0)
        def _():
            halo_copy(par, 1).start()

    def communicate(n, par):
        for pc in range(2):
            for part in range(len(PARTS)):
                rows = pl.ds(*PARTS[part])
                rs_copy(pc, part, 0).wait_recv()
                rs_copy(pc, part, 1).wait_recv()
                at = near(-2)
                rho[pc, at, rows] = rho[pc, at, rows] + rsbuf[pc, 0, rows] + rsbuf[pc, 1, rows]
                rs_copy(pc, part, 5).start()
                rs_copy(pc, part, 2).wait_recv()
                at = near(2)
                rho[pc, at, rows] = rho[pc, at, rows] + rsbuf[pc, 2, rows]
                rs_copy(pc, part, 6).start()
            if pc == 0:
                send_direct(1)
        below = jnp.zeros((4, LANES), F32)
        above = jnp.zeros((4, LANES), F32)
        whole_in = ca_src[0]
        whole_out = ca_src[1]
        for k in range(1, ng):
            ca_copy(par, k).wait_recv()
            peer = lax.rem(g - k + ng, ng)
            got_in = ca_buf[par, k - 1, 0]
            got_out = ca_buf[par, k - 1, 1]
            below = below + got_in * jnp.where(peer < g, 1.0, 0.0).astype(F32)
            above = above + got_out * jnp.where(peer > g, 1.0, 0.0).astype(F32)
            whole_in = whole_in + got_in
            whole_out = whole_out + got_out
        cb_src[0] = whole_in
        cb_src[1] = whole_out
        for k in range(1, ny):
            cb_copy(par, k).start()

        quarter = lax.rem(lax.div(z, 2), 2)
        for pc in range(2):
            tile = 2 * pc + lax.rem(z, 2)
            for part in range(len(PARTS)):
                size = PARTS[part][1]
                rows = pl.ds(*PARTS[part])
                for i in (3, 4, 5, 6):
                    rs_copy(pc, part, i).wait_recv()
                acc = (rho[pc, z, rows] + rsbuf[pc, 3, rows]) + (
                    rsbuf[pc, 4, rows] + rsbuf[pc, 5, rows]
                )
                acc = (acc + rsbuf[pc, 6, rows]) * delta
                up = up_t[tile, quarter, rows]
                dn = dn_t[tile, quarter, rows]

                pair = jnp.concatenate([acc * up, acc * dn], axis=1)
                hi = pair.astype(BF16).astype(F32)
                sums = dot(jnp.concatenate([hi, pair - hi], axis=0).astype(BF16), tri)
                sums = sums[:size] + sums[size:]
                pot[pc, z, rows] = dn * sums[:, :LANES] + up * sums[:, LANES:]
                for i in (0, 1):
                    ag_copy(pc, part, i).start()
            if pc == 0:
                for part in range(len(PARTS)):
                    for i in (2, 3):
                        ag_copy(pc, part, i).start()
        for k in range(1, ny):
            cb_copy(par, k).wait_recv()
            peer = lax.rem(y - k + ny, ny)
            below = below + cb_buf[par, k - 1, 0] * jnp.where(peer < y, 1.0, 0.0).astype(F32)
            above = above + cb_buf[par, k - 1, 1] * jnp.where(peer > y, 1.0, 0.0).astype(F32)
        far = own[8:12]
        cc_src[0] = jnp.where(lane4 < half, below, pltpu.roll(far, half, 1))
        cc_src[1] = jnp.where(lane4 < half, above, pltpu.roll(far, 2 * half - LANES, 1))
        for k in range(1, nz):
            cc_copy(par, k).start()

        @pl.when(r < nr - 1)
        def _():
            halo_copy(par, 0).wait_send()
            halo_copy(par, 1).wait_recv()

        @pl.when(r > 0)
        def _():
            halo_copy(par, 1).wait_send()
            halo_copy(par, 0).wait_recv()

        prepare(n, par, 0)
        for pc in range(2):
            for part in range(len(PARTS)):
                ag_copy(pc, part, 0).wait_recv()
                ag_copy(pc, part, 4).start()
                ag_copy(pc, part, 5).start()
                ag_copy(pc, part, 1).wait_recv()
                ag_copy(pc, part, 6).start()
            if pc == 0:
                for part in range(len(PARTS)):
                    for i in (2, 3):
                        ag_copy(1, part, i).start()
        prepare(n, par, 1)
        carry = [cc_src[kind] for kind in range(2)]
        for k in range(1, nz):
            cc_copy(par, k).wait_recv()
            carry = [carry[kind] + cc_buf[par, k - 1, kind] for kind in range(2)]
        for pc in range(2):
            for part in range(len(PARTS)):
                for i in range(7):
                    rs_copy(pc, part, i).wait_send()
        for k in range(1, ng):
            ca_copy(par, k).wait_send()
        for k in range(1, ny):
            cb_copy(par, k).wait_send()
        for k in range(1, nz):
            cc_copy(par, k).wait_send()

        first = pltpu.roll(carry[0], LANES - half, 1)
        second = pltpu.roll(carry[1], 2 * LANES - 2 * half, 1)
        far = jnp.where(lane4 < LANES - half, first, second)
        own[0:4] = carry[0]
        own[4:8] = carry[1] + far
        own[8:12] = carry[1]
        pad = jnp.zeros((LANES - 16, LANES), F32)
        return jnp.transpose(jnp.concatenate([own[...], pad], axis=0))[:half]

    def advance(n, par, pc, carry):
        base = pc * 2 * LANES
        for part in range(len(PARTS)):
            for i in (2, 3, 4, 5, 6):
                ag_copy(pc, part, i).wait_recv()
        for p in range(2):
            cols = [[], []]
            for mh in range(2):
                k = 2 * p + mh
                t = 2 * pc
                first_pot = pot[pc, 4 * p + 2 * mh]
                second_pot = pot[pc, 4 * p + 2 * mh + 1]
                wide = (half, LANES)
                below = jnp.broadcast_to(carry[:, k : k + 1], wide)
                at = 4 * (pc + 1) + k
                above = jnp.broadcast_to(carry[:, at : at + 1], wide)
                in_first = jnp.broadcast_to(first_pot[:, LANES - 1 :], wide) * sc_in[t, mh]
                out_second = jnp.broadcast_to(second_pot[:, :1], wide) * sc_out[t + 1, mh]
                if pc == 0:
                    in_second = jnp.broadcast_to(second_pot[:, LANES - 1 :], wide)
                    tin01[k] = in_first + in_second * sc_in[t + 1, mh]
                else:
                    below = below + tin01[k]
                cols[0].append(
                    first_pot + dn_t[t, mh] * below + up_t[t, mh] * (above + out_second)
                )
                cols[1].append(
                    second_pot + dn_t[t + 1, mh] * (below + in_first) + up_t[t + 1, mh] * above
                )
            cols = [jnp.concatenate(parts, axis=0) for parts in cols]
            hi, lo = split2(jnp.concatenate(cols, axis=1))
            wide = dot(f_both[...], hi)
            field[pc, p] = wide[:chans] + (wide[chans:] + dot(f_both[:chans], lo))
        factor = jnp.where(n == 0, 2.0, 1.0).astype(F32)
        lanes = slice(base, base + 2 * LANES)
        for c0 in range(0, chans, ROWS_STEP):
            rows = slice(c0, c0 + ROWS_STEP)
            al = alpha[rows, lanes] * factor
            be = beta[rows, lanes] * factor
            ob = orb[rows, lanes]
            f0 = field[pc, 0, rows]
            f1 = field[pc, 1, rows]
            new = (
                known[0, rows, lanes] + (al * f1 - be * f0),
                known[1, rows, lanes] - (al * f0 + be * f1),
            )
            for p in range(2):
                vbuf[1 - par, p, rows, pl.ds(LANES + base, 2 * LANES)] = new[p]
                hi, lo = split2(new[p] * ob)
                w_hi[p, rows] = hi
                w_lo[p, rows] = lo

    loads[0].wait()
    loads[1].wait()
    spread_orbitals()
    loads[2].wait()
    weigh(0, 0)
    loads[3].wait()
    split_density()
    densities(0)
    pl.semaphore_wait(barrier, 4 + (ng - 1) + (ny - 1) + 2)
    send_far(0)
    send_direct(0)
    weigh(0, 1)
    densities(1)
    send_far(1)
    loads[4].wait()
    power_tables()
    totals()
    send_totals(0)
    loads[5].wait()
    loads[6].wait()
    diagonal_tables()

    def store(pc):
        at = pc * 2 * LANES
        return pltpu.make_async_copy(
            vbuf.at[SWEEPS % 2, :, :, pl.ds(LANES + at, 2 * LANES)],
            out_hbm.at[:, :, pl.ds(at, 2 * LANES)],
            io_sem.at[pc],
        )

    def sweep(n, c):
        par = lax.rem(n, 2)
        carry = communicate(n, par)
        for pc in range(2):
            advance(n, par, pc, carry)

            @pl.when(n < SWEEPS - 1)
            def _():
                densities(pc)

            for part in range(len(PARTS)):
                for i in range(7):
                    ag_copy(pc, part, i).wait_send()

            @pl.when(n < SWEEPS - 1)
            def _():
                send_far(pc)
                if pc == 0:
                    send_direct(0)

            @pl.when(n == SWEEPS - 1)
            def _():
                store(pc).start()

        @pl.when(n < SWEEPS - 1)
        def _():
            totals()
            send_totals(1 - par)

        return c

    lax.fori_loop(0, SWEEPS, sweep, 0)
    for pc in range(2):
        store(pc).wait()


def body(nz, nr, wavefunc, orbitals, channel_orbital, channel_l, row_order, density, coupling):
    chans, width = wavefunc.shape[1:]
    rows = row_order.shape[0]
    half = rows // 2
    ng = 8 if nr % 8 == 0 else 2
    ny = nr // ng
    hbm = pl.BlockSpec(memory_space=pl.ANY)
    dma = pltpu.SemaphoreType.DMA
    scratch = [
        pltpu.VMEM(orbitals.shape, F32),
        pltpu.VMEM((1, chans), jnp.int32),
        pltpu.VMEM((1, chans), jnp.int32),
        pltpu.VMEM((1, rows), jnp.int32),
        pltpu.VMEM((rows, chans), F32),
        pltpu.VMEM((rows, chans), F32),
        pltpu.VMEM((2, 2, chans, width + 2 * LANES), F32),
        pltpu.VMEM((2, chans, width), F32),
        pltpu.VMEM((chans, width), F32),
        pltpu.VMEM((chans, width), F32),
        pltpu.VMEM((chans, width), F32),
        pltpu.VMEM((2, chans, width), F32),
        pltpu.VMEM((chans, width), F32),
        pltpu.VMEM((chans, width), F32),
        pltpu.VMEM((2, 2, chans, 2 * LANES), F32),
        pltpu.VMEM((2, chans, 2 * LANES), BF16),
        pltpu.VMEM((2, chans, 2 * LANES), BF16),
        pltpu.VMEM((4, 2, half, LANES), F32),
        pltpu.VMEM((4, 2, half, LANES), F32),
        pltpu.VMEM((2 * rows, chans), BF16),
        pltpu.VMEM((2 * chans, rows), BF16),
        pltpu.VMEM((2, 8, half, LANES), F32),
        pltpu.VMEM((2, 8, half, LANES), F32),
        pltpu.VMEM((2, 7, half, LANES), F32),
        pltpu.VMEM((16, LANES), F32),
        pltpu.VMEM((4, half, LANES), F32),
        pltpu.VMEM((4, 2, half, LANES), F32),
        pltpu.VMEM((4, 2, half, LANES), F32),
        pltpu.VMEM((2, 4, LANES), F32),
        pltpu.VMEM((2, ng - 1, 2, 4, LANES), F32),
        pltpu.VMEM((2, 4, LANES), F32),
        pltpu.VMEM((2, ny - 1, 2, 4, LANES), F32),
        pltpu.VMEM((2, 4, LANES), F32),
        pltpu.VMEM((2, nz - 1, 2, 4, LANES), F32),
        dma((7,)),
        dma((2, len(PARTS), 7)),
        dma((2, len(PARTS), 7)),
        dma((2, len(PARTS), 7)),
        dma((2, len(PARTS), 7)),
        dma((ng - 1,)),
        dma((2, ng - 1)),
        dma((ny - 1,)),
        dma((2, ny - 1)),
        dma((nz - 1,)),
        dma((2, nz - 1)),
        dma((2,)),
        dma((2, 2)),
    ]
    return pl.pallas_call(
        functools.partial(kernel, (nz, nr, ng, chans, width, half)),
        out_shape=jax.ShapeDtypeStruct(wavefunc.shape, F32),
        in_specs=[hbm] * 7,
        out_specs=hbm,
        scratch_shapes=scratch,
        compiler_params=pltpu.CompilerParams(
            collective_id=0, has_side_effects=True, vmem_limit_bytes=48 << 20
        ),
        name="cn_step",
    )(
        *(
            pltpu.with_memory_space_constraint(x, pltpu.HBM)
            for x in (
                wavefunc,
                orbitals,
                channel_orbital.reshape(1, chans),
                channel_l.reshape(1, chans),
                row_order.reshape(1, rows),
                density,
                coupling.T,
            )
        )
    )


def solution(mesh):
    placed = (
        P(None, "chan", "rad"),
        P(None, "rad"),
        P("chan"),
        P("chan"),
        P(),
        P(None, "chan"),
        P("chan", None),
    )
    return jax.shard_map(
        functools.partial(body, mesh.shape["chan"], mesh.shape["rad"]),
        mesh=mesh,
        in_specs=placed,
        out_specs=P(None, "chan", "rad"),
        check_vma=False,
    )
```

```python
import functools

import jax
import jax.numpy as jnp
from jax import lax
from jax.experimental import pallas as pl
from jax.experimental.pallas import tpu as pltpu
from jax.sharding import PartitionSpec as P

SWEEPS = 4
MESH = pl.DeviceIdType.MESH
F32 = jnp.float32
BF16 = jnp.bfloat16
LANES = 128
SPAN = 400.0 / 408.0

RS_PLAN = ((-4, -2), (-3, -1), (3, 1), (-1, -1), (1, 1), (-2, -2), (2, 2))
AG_PLAN = ((0, 2), (0, -2), (0, 1), (0, -1), (-2, 2), (-2, 1), (2, -1))
PARTS = ((0, 40), (40, 32))
WHOLE = (0, 72)
RS_WHOLE = (3, 4)
AG_WHOLE = (2, 3)
ROWS_STEP = 32


def split2(x):
    hi = x.astype(BF16)
    return hi, (x - hi.astype(F32)).astype(BF16)


def dot(a, b):
    return jnp.dot(a, b, preferred_element_type=F32)


def as_column(row):
    eight = jnp.broadcast_to(row, (8, row.shape[1]))
    first = lax.broadcasted_iota(jnp.int32, (8, LANES), 0) == 0
    return lax.dot_general(
        eight,
        jnp.where(first, 1.0, 0.0).astype(F32),
        (((0,), (0,)), ((), ())),
        precision=lax.Precision.HIGHEST,
        preferred_element_type=F32,
    )


def kernel(
    sizes,
    wave_hbm,
    orbitals_hbm,
    which_hbm,
    ell_hbm,
    order_hbm,
    density_hbm,
    coupling_hbm,
    out_hbm,
    orbitals_ref,
    which_ref,
    ell_ref,
    order_ref,
    density_ref,
    coupling_ref,
    vbuf,
    rhs,
    orb,
    diag,
    scl,
    known,
    alpha,
    beta,
    field,
    w_hi,
    w_lo,
    up_t,
    dn_t,
    d_both,
    f_both,
    rho,
    pot,
    rsbuf,
    own,
    tin01,
    sc_in,
    sc_out,
    ca_src,
    ca_buf,
    cb_src,
    cb_buf,
    cc_src,
    cc_buf,
    io_sem,
    rs_s,
    rs_r,
    ag_s,
    ag_r,
    ca_s,
    ca_r,
    cb_s,
    cb_r,
    cc_s,
    cc_r,
    ha_s,
    ha_r,
):
    nz, nr, ng, chans, width, half = sizes
    ny = nr // ng
    z = lax.axis_index("chan")
    r = lax.axis_index("rad")
    g = lax.rem(r, ng)
    y = lax.div(r, ng)
    total_rows = width * nr
    delta = SPAN / total_rows

    def zdev(offset):
        return (lax.rem(z + offset + nz, nz), r)

    sign = 1 - 2 * lax.rem(r, 2)

    def near(offset):
        return lax.rem(z + sign * offset + nz, nz)

    def gdev(k):
        return (z, y * ng + lax.rem(g + k, ng))

    def ydev(k):
        return (z, lax.rem(y + k, ny) * ng + g)

    barrier = pltpu.get_barrier_semaphore()

    def greet(device):
        pl.semaphore_signal(barrier, inc=1, device_id=device, device_id_type=MESH)

    for k in (1, 2, nz - 2, nz - 1):
        greet(zdev(k))
    for k in range(1, ng):
        greet(gdev(k))
    for k in range(1, ny):
        greet(ydev(k))
    greet((z, lax.rem(r + 1, nr)))
    greet((z, lax.rem(r + nr - 1, nr)))

    loads = [
        pltpu.make_async_copy(src, dst, io_sem.at[i])
        for i, (src, dst) in enumerate(
            (
                (which_hbm, which_ref),
                (orbitals_hbm, orbitals_ref),
                (wave_hbm, vbuf.at[0, :, :, pl.ds(LANES, width)]),
                (density_hbm, density_ref),
                (order_hbm, order_ref),
                (ell_hbm, ell_ref),
                (coupling_hbm, coupling_ref),
            )
        )
    ]
    for load in loads:
        load.start()

    @pl.when(r == 0)
    def _():
        for par in range(2):
            for p in range(2):
                vbuf[par, p, :, 0:LANES] = jnp.zeros((chans, LANES), F32)

    @pl.when(r == nr - 1)
    def _():
        for par in range(2):
            for p in range(2):
                vbuf[par, p, :, LANES + width :] = jnp.zeros((chans, LANES), F32)

    tiles = width // LANES
    i0 = lax.broadcasted_iota(jnp.int32, (2 * LANES, 2 * LANES), 0)
    i1 = lax.broadcasted_iota(jnp.int32, (2 * LANES, 2 * LANES), 1)
    inner = (i0 < LANES) & (i1 < LANES) & (i0 <= i1)
    outer = (i0 >= LANES) & (i1 >= LANES) & (i0 > i1)
    tri = jnp.where(inner | outer, 1.0, 0.0).astype(BF16)
    lane4 = lax.broadcasted_iota(jnp.int32, (4, LANES), 1)
    lane_id = lax.broadcasted_iota(jnp.int32, (half, LANES), 1)

    def spread_orbitals():
        which = as_column(which_ref[...].astype(F32))
        for t in range(tiles):
            lanes = slice(t * LANES, (t + 1) * LANES)
            for c0 in range(0, chans, ROWS_STEP):
                rows = slice(c0, c0 + ROWS_STEP)
                pick = which[rows]
                value = jnp.zeros((ROWS_STEP, LANES), F32)
                for o in range(orbitals_ref.shape[0]):
                    value = jnp.where(pick == float(o), orbitals_ref[o : o + 1, lanes], value)
                orb[rows, lanes] = value

    def split_density():
        hi, lo = split2(density_ref[...])
        d_both[: 2 * half] = hi
        d_both[2 * half :] = lo

    def radius_of(t):
        lane = lax.broadcasted_iota(jnp.int32, (1, LANES), 1)
        index = (r * width + t * LANES + lane).astype(F32)
        return 8.0 + 400.0 * (index + 0.5) / total_rows

    def power_tables():
        order = as_column(order_ref[...].astype(F32))
        for t in range(tiles):
            scaled = radius_of(t) / 408.0
            up = jnp.exp(order * jnp.log(scaled))
            dn = 1.0 / (up * scaled)
            inv_dn = jnp.broadcast_to((up * scaled)[:, LANES - 1 :], up.shape)
            inv_up = jnp.broadcast_to((dn * scaled)[:, :1], up.shape)
            for mh in range(2):
                rows = slice(mh * half, (mh + 1) * half)
                up_t[t, mh] = up[rows]
                dn_t[t, mh] = dn[rows]
                sc_in[t, mh] = inv_dn[rows]
                sc_out[t, mh] = inv_up[rows]

    def diagonal_tables():
        ell = as_column(ell_ref[...].astype(F32))
        strength = ell * (ell + 1.0)
        for t in range(tiles):
            radius = radius_of(t)
            inv = 1.0 / (4.0 * radius * radius)
            lanes = slice(t * LANES, (t + 1) * LANES)
            for c0 in range(0, chans, ROWS_STEP):
                rows = slice(c0, c0 + ROWS_STEP)
                dg = 0.5 + strength[rows] * inv
                sc = 1.0 / (1.0 + dg * dg)
                al = sc * orb[rows, lanes]
                diag[rows, lanes] = dg
                scl[rows, lanes] = sc
                alpha[rows, lanes] = al
                beta[rows, lanes] = al * dg
        turned = jnp.concatenate(
            [coupling_ref[...], jnp.zeros((chans - 2 * half, chans), F32)], axis=0
        )
        hi, lo = split2(jnp.transpose(turned)[:, : 2 * half])
        f_both[:chans] = hi
        f_both[chans:] = lo

    def rs_copy(pc, part, i):
        chunk, target = RS_PLAN[i]
        rows = pl.ds(*(WHOLE if i in RS_WHOLE else PARTS[part]))
        return pltpu.make_async_remote_copy(
            src_ref=rho.at[pc, near(chunk), rows],
            dst_ref=rsbuf.at[pc, i, rows],
            send_sem=rs_s.at[pc, part, i],
            recv_sem=rs_r.at[pc, part, i],
            device_id=(near(target), r),
            device_id_type=MESH,
        )

    def ag_copy(pc, part, i):
        chunk, target = AG_PLAN[i]
        rows = pl.ds(*(WHOLE if i in AG_WHOLE else PARTS[part]))
        place = pot.at[pc, near(chunk), rows]
        return pltpu.make_async_remote_copy(
            src_ref=place,
            dst_ref=place,
            send_sem=ag_s.at[pc, part, i],
            recv_sem=ag_r.at[pc, part, i],
            device_id=(near(target), r),
            device_id_type=MESH,
        )

    def small_copy(src, buf, send, recv, par, k, device):
        return pltpu.make_async_remote_copy(
            src_ref=src,
            dst_ref=buf.at[par, k - 1],
            send_sem=send.at[k - 1],
            recv_sem=recv.at[par, k - 1],
            device_id=device,
            device_id_type=MESH,
        )

    def ca_copy(par, k):
        return small_copy(ca_src, ca_buf, ca_s, ca_r, par, k, gdev(k))

    def cb_copy(par, k):
        return small_copy(cb_src, cb_buf, cb_s, cb_r, par, k, ydev(k))

    def cc_copy(par, k):
        return small_copy(cc_src, cc_buf, cc_s, cc_r, par, k, zdev(k))

    def halo_copy(par, side):
        here, there = (width, 0) if side == 0 else (LANES, LANES + width)
        to = r + 1 if side == 0 else r - 1
        to = lax.rem(to + nr, nr)
        return pltpu.make_async_remote_copy(
            src_ref=vbuf.at[par, :, :, pl.ds(here, LANES)],
            dst_ref=vbuf.at[par, :, :, pl.ds(there, LANES)],
            send_sem=ha_s.at[side],
            recv_sem=ha_r.at[par, side],
            device_id=(z, to),
            device_id_type=MESH,
        )

    def weigh(par, pc):
        lanes = slice(pc * 2 * LANES, (pc + 1) * 2 * LANES)
        for c0 in range(0, chans, ROWS_STEP):
            rows = slice(c0, c0 + ROWS_STEP)
            for p in range(2):
                v = vbuf[par, p, rows, LANES + lanes.start : LANES + lanes.stop]
                hi, lo = split2(v * orb[rows, lanes])
                w_hi[p, rows] = hi
                w_lo[p, rows] = lo

    def densities(pc):
        rows = 2 * half
        for p in range(2):
            wide = dot(d_both[...], w_hi[p])
            part = wide[:rows] + (wide[rows:] + dot(d_both[:rows], w_lo[p]))
            for mh in range(2):
                for h in range(2):
                    rho[pc, 4 * p + 2 * mh + h] = part[
                        mh * half : (mh + 1) * half, h * LANES : (h + 1) * LANES
                    ]

    def prepare(n, par, pc):
        base = pc * 2 * LANES
        lanes = slice(base, base + 2 * LANES)

        def kinetic(rows):
            v, kin = [], []
            for p in range(2):
                x = vbuf[par, p, rows, pl.ds(base, 4 * LANES)]
                left = pltpu.roll(x, 1, 1)[:, LANES : 3 * LANES]
                right = pltpu.roll(x, 4 * LANES - 1, 1)[:, LANES : 3 * LANES]
                v.append(x[:, LANES : 3 * LANES])
                kin.append(-0.25 * (left + right))
            return v, kin

        @pl.when(n == 0)
        def _():
            for c0 in range(0, chans, ROWS_STEP):
                rows = slice(c0, c0 + ROWS_STEP)
                v, kin = kinetic(rows)
                dg = diag[rows, lanes]
                rhs[0, rows, lanes] = v[0] + (kin[1] + dg * v[1])
                rhs[1, rows, lanes] = v[1] - (kin[0] + dg * v[0])

        @pl.when(n == 1)
        def _():
            for c0 in range(0, chans, ROWS_STEP):
                rows = slice(c0, c0 + ROWS_STEP)
                ob = orb[rows, lanes]
                rhs[0, rows, lanes] = rhs[0, rows, lanes] + field[pc, 1, rows] * ob
                rhs[1, rows, lanes] = rhs[1, rows, lanes] - field[pc, 0, rows] * ob

        for c0 in range(0, chans, ROWS_STEP):
            rows = slice(c0, c0 + ROWS_STEP)
            v, kin = kinetic(rows)
            dg = diag[rows, lanes]
            sc = scl[rows, lanes]
            q0 = rhs[0, rows, lanes] + kin[1]
            q1 = rhs[1, rows, lanes] - kin[0]
            known[0, rows, lanes] = (q0 + dg * q1) * sc
            known[1, rows, lanes] = (q1 - dg * q0) * sc

    def send_far(pc):
        for part in range(len(PARTS)):
            for i in (0, 1, 2):
                rs_copy(pc, part, i).start()

    def send_direct(pc):
        for i in RS_WHOLE:
            rs_copy(pc, 0, i).start()

    def totals():
        acc = jnp.zeros((half, LANES), F32)
        for p in range(2):
            for mh in range(2):
                blocks = [rho[t // 2, 4 * p + 2 * mh + t % 2] * delta for t in range(tiles)]
                ups = [blocks[t] * up_t[t, mh] for t in range(tiles)]
                dns = [blocks[t] * dn_t[t, mh] for t in range(tiles)]
                near_out = dns[0] + dns[1]
                far_out = dns[2] + dns[3]
                sums = ((ups[0] + ups[1]) + (ups[2] + ups[3]), near_out + far_out, far_out)
                for kind in range(3):
                    s = jnp.sum(sums[kind], axis=1, keepdims=True)
                    acc = jnp.where(lane_id == kind * 4 + p * 2 + mh, s, acc)
        full = jnp.concatenate([acc, jnp.zeros((LANES - half, LANES), F32)], axis=0)
        own[...] = jnp.transpose(full)[0:16]
        ca_src[0] = own[0:4]
        ca_src[1] = own[4:8]

    def send_totals(par):
        for k in range(1, ng):
            ca_copy(par, k).start()

        @pl.when(r < nr - 1)
        def _():
            halo_copy(par, 0).start()

        @pl.when(r > 0)
        def _():
            halo_copy(par, 1).start()

    def communicate(n, par):
        for pc in range(2):
            for part in range(len(PARTS)):
                rows = pl.ds(*PARTS[part])
                rs_copy(pc, part, 0).wait_recv()
                rs_copy(pc, part, 1).wait_recv()
                at = near(-2)
                rho[pc, at, rows] = rho[pc, at, rows] + rsbuf[pc, 0, rows] + rsbuf[pc, 1, rows]
                rs_copy(pc, part, 5).start()
                rs_copy(pc, part, 2).wait_recv()
                at = near(2)
                rho[pc, at, rows] = rho[pc, at, rows] + rsbuf[pc, 2, rows]
                rs_copy(pc, part, 6).start()
            if pc == 0:
                send_direct(1)
        below = jnp.zeros((4, LANES), F32)
        above = jnp.zeros((4, LANES), F32)
        whole_in = ca_src[0]
        whole_out = ca_src[1]
        for k in range(1, ng):
            ca_copy(par, k).wait_recv()
            peer = lax.rem(g - k + ng, ng)
            got_in = ca_buf[par, k - 1, 0]
            got_out = ca_buf[par, k - 1, 1]
            below = below + got_in * jnp.where(peer < g, 1.0, 0.0).astype(F32)
            above = above + got_out * jnp.where(peer > g, 1.0, 0.0).astype(F32)
            whole_in = whole_in + got_in
            whole_out = whole_out + got_out
        cb_src[0] = whole_in
        cb_src[1] = whole_out
        for k in range(1, ny):
            cb_copy(par, k).start()

        quarter = lax.rem(lax.div(z, 2), 2)
        for pc in range(2):
            tile = 2 * pc + lax.rem(z, 2)
            for part in range(len(PARTS)):
                size = PARTS[part][1]
                rows = pl.ds(*PARTS[part])
                for i in (5, 6) if part else (3, 4, 5, 6):
                    rs_copy(pc, part, i).wait_recv()
                acc = (rho[pc, z, rows] + rsbuf[pc, 3, rows]) + (
                    rsbuf[pc, 4, rows] + rsbuf[pc, 5, rows]
                )
                acc = (acc + rsbuf[pc, 6, rows]) * delta
                up = up_t[tile, quarter, rows]
                dn = dn_t[tile, quarter, rows]

                pair = jnp.concatenate([acc * up, acc * dn], axis=1)
                hi = pair.astype(BF16).astype(F32)
                sums = dot(jnp.concatenate([hi, pair - hi], axis=0).astype(BF16), tri)
                sums = sums[:size] + sums[size:]
                pot[pc, z, rows] = dn * sums[:, :LANES] + up * sums[:, LANES:]
                for i in (0, 1):
                    ag_copy(pc, part, i).start()
            if pc == 0:
                for i in AG_WHOLE:
                    ag_copy(pc, 0, i).start()
        for k in range(1, ny):
            cb_copy(par, k).wait_recv()
            peer = lax.rem(y - k + ny, ny)
            below = below + cb_buf[par, k - 1, 0] * jnp.where(peer < y, 1.0, 0.0).astype(F32)
            above = above + cb_buf[par, k - 1, 1] * jnp.where(peer > y, 1.0, 0.0).astype(F32)
        far = own[8:12]
        cc_src[0] = jnp.where(lane4 < half, below, pltpu.roll(far, half, 1))
        cc_src[1] = jnp.where(lane4 < half, above, pltpu.roll(far, 2 * half - LANES, 1))
        for k in range(1, nz):
            cc_copy(par, k).start()

        @pl.when(r < nr - 1)
        def _():
            halo_copy(par, 0).wait_send()
            halo_copy(par, 1).wait_recv()

        @pl.when(r > 0)
        def _():
            halo_copy(par, 1).wait_send()
            halo_copy(par, 0).wait_recv()

        prepare(n, par, 0)
        for pc in range(2):
            for part in range(len(PARTS)):
                ag_copy(pc, part, 0).wait_recv()
                ag_copy(pc, part, 4).start()
                ag_copy(pc, part, 5).start()
                ag_copy(pc, part, 1).wait_recv()
                ag_copy(pc, part, 6).start()
            if pc == 0:
                for i in AG_WHOLE:
                    ag_copy(1, 0, i).start()
        prepare(n, par, 1)
        carry = [cc_src[kind] for kind in range(2)]
        for k in range(1, nz):
            cc_copy(par, k).wait_recv()
            carry = [carry[kind] + cc_buf[par, k - 1, kind] for kind in range(2)]
        for pc in range(2):
            for part in range(len(PARTS)):
                for i in range(7):
                    if part == 0 or i not in RS_WHOLE:
                        rs_copy(pc, part, i).wait_send()
        for k in range(1, ng):
            ca_copy(par, k).wait_send()
        for k in range(1, ny):
            cb_copy(par, k).wait_send()
        for k in range(1, nz):
            cc_copy(par, k).wait_send()

        first = pltpu.roll(carry[0], LANES - half, 1)
        second = pltpu.roll(carry[1], 2 * LANES - 2 * half, 1)
        far = jnp.where(lane4 < LANES - half, first, second)
        own[0:4] = carry[0]
        own[4:8] = carry[1] + far
        own[8:12] = carry[1]
        pad = jnp.zeros((LANES - 16, LANES), F32)
        return jnp.transpose(jnp.concatenate([own[...], pad], axis=0))[:half]

    def advance(n, par, pc, carry):
        base = pc * 2 * LANES
        for part in range(len(PARTS)):
            for i in (4, 5, 6) if part else (2, 3, 4, 5, 6):
                ag_copy(pc, part, i).wait_recv()
        for p in range(2):
            cols = [[], []]
            for mh in range(2):
                k = 2 * p + mh
                t = 2 * pc
                first_pot = pot[pc, 4 * p + 2 * mh]
                second_pot = pot[pc, 4 * p + 2 * mh + 1]
                wide = (half, LANES)
                below = jnp.broadcast_to(carry[:, k : k + 1], wide)
                at = 4 * (pc + 1) + k
                above = jnp.broadcast_to(carry[:, at : at + 1], wide)
                in_first = jnp.broadcast_to(first_pot[:, LANES - 1 :], wide) * sc_in[t, mh]
                out_second = jnp.broadcast_to(second_pot[:, :1], wide) * sc_out[t + 1, mh]
                if pc == 0:
                    in_second = jnp.broadcast_to(second_pot[:, LANES - 1 :], wide)
                    tin01[k] = in_first + in_second * sc_in[t + 1, mh]
                else:
                    below = below + tin01[k]
                cols[0].append(
                    first_pot + dn_t[t, mh] * below + up_t[t, mh] * (above + out_second)
                )
                cols[1].append(
                    second_pot + dn_t[t + 1, mh] * (below + in_first) + up_t[t + 1, mh] * above
                )
            cols = [jnp.concatenate(parts, axis=0) for parts in cols]
            hi, lo = split2(jnp.concatenate(cols, axis=1))
            wide = dot(f_both[...], hi)
            field[pc, p] = wide[:chans] + (wide[chans:] + dot(f_both[:chans], lo))
        factor = jnp.where(n == 0, 2.0, 1.0).astype(F32)
        lanes = slice(base, base + 2 * LANES)
        for c0 in range(0, chans, ROWS_STEP):
            rows = slice(c0, c0 + ROWS_STEP)
            al = alpha[rows, lanes] * factor
            be = beta[rows, lanes] * factor
            ob = orb[rows, lanes]
            f0 = field[pc, 0, rows]
            f1 = field[pc, 1, rows]
            new = (
                known[0, rows, lanes] + (al * f1 - be * f0),
                known[1, rows, lanes] - (al * f0 + be * f1),
            )
            for p in range(2):
                vbuf[1 - par, p, rows, pl.ds(LANES + base, 2 * LANES)] = new[p]
                hi, lo = split2(new[p] * ob)
                w_hi[p, rows] = hi
                w_lo[p, rows] = lo

    loads[0].wait()
    loads[1].wait()
    spread_orbitals()
    loads[2].wait()
    weigh(0, 0)
    loads[3].wait()
    split_density()
    densities(0)
    pl.semaphore_wait(barrier, 4 + (ng - 1) + (ny - 1) + 2)
    send_far(0)
    send_direct(0)
    weigh(0, 1)
    densities(1)
    send_far(1)
    loads[4].wait()
    power_tables()
    totals()
    send_totals(0)
    loads[5].wait()
    loads[6].wait()
    diagonal_tables()

    def store(pc):
        at = pc * 2 * LANES
        return pltpu.make_async_copy(
            vbuf.at[SWEEPS % 2, :, :, pl.ds(LANES + at, 2 * LANES)],
            out_hbm.at[:, :, pl.ds(at, 2 * LANES)],
            io_sem.at[pc],
        )

    def sweep(n, c):
        par = lax.rem(n, 2)
        carry = communicate(n, par)
        for pc in range(2):
            advance(n, par, pc, carry)

            @pl.when(n < SWEEPS - 1)
            def _():
                densities(pc)

            for part in range(len(PARTS)):
                for i in range(7):
                    if part == 0 or i not in AG_WHOLE:
                        ag_copy(pc, part, i).wait_send()

            @pl.when(n < SWEEPS - 1)
            def _():
                send_far(pc)
                if pc == 0:
                    send_direct(0)

            @pl.when(n == SWEEPS - 1)
            def _():
                store(pc).start()

        @pl.when(n < SWEEPS - 1)
        def _():
            totals()
            send_totals(1 - par)

        return c

    lax.fori_loop(0, SWEEPS, sweep, 0)
    for pc in range(2):
        store(pc).wait()


def body(nz, nr, wavefunc, orbitals, channel_orbital, channel_l, row_order, density, coupling):
    chans, width = wavefunc.shape[1:]
    rows = row_order.shape[0]
    half = rows // 2
    ng = 8 if nr % 8 == 0 else 2
    ny = nr // ng
    hbm = pl.BlockSpec(memory_space=pl.ANY)
    dma = pltpu.SemaphoreType.DMA
    scratch = [
        pltpu.VMEM(orbitals.shape, F32),
        pltpu.VMEM((1, chans), jnp.int32),
        pltpu.VMEM((1, chans), jnp.int32),
        pltpu.VMEM((1, rows), jnp.int32),
        pltpu.VMEM((rows, chans), F32),
        pltpu.VMEM((rows, chans), F32),
        pltpu.VMEM((2, 2, chans, width + 2 * LANES), F32),
        pltpu.VMEM((2, chans, width), F32),
        pltpu.VMEM((chans, width), F32),
        pltpu.VMEM((chans, width), F32),
        pltpu.VMEM((chans, width), F32),
        pltpu.VMEM((2, chans, width), F32),
        pltpu.VMEM((chans, width), F32),
        pltpu.VMEM((chans, width), F32),
        pltpu.VMEM((2, 2, chans, 2 * LANES), F32),
        pltpu.VMEM((2, chans, 2 * LANES), BF16),
        pltpu.VMEM((2, chans, 2 * LANES), BF16),
        pltpu.VMEM((4, 2, half, LANES), F32),
        pltpu.VMEM((4, 2, half, LANES), F32),
        pltpu.VMEM((2 * rows, chans), BF16),
        pltpu.VMEM((2 * chans, rows), BF16),
        pltpu.VMEM((2, 8, half, LANES), F32),
        pltpu.VMEM((2, 8, half, LANES), F32),
        pltpu.VMEM((2, 7, half, LANES), F32),
        pltpu.VMEM((16, LANES), F32),
        pltpu.VMEM((4, half, LANES), F32),
        pltpu.VMEM((4, 2, half, LANES), F32),
        pltpu.VMEM((4, 2, half, LANES), F32),
        pltpu.VMEM((2, 4, LANES), F32),
        pltpu.VMEM((2, ng - 1, 2, 4, LANES), F32),
        pltpu.VMEM((2, 4, LANES), F32),
        pltpu.VMEM((2, ny - 1, 2, 4, LANES), F32),
        pltpu.VMEM((2, 4, LANES), F32),
        pltpu.VMEM((2, nz - 1, 2, 4, LANES), F32),
        dma((7,)),
        dma((2, len(PARTS), 7)),
        dma((2, len(PARTS), 7)),
        dma((2, len(PARTS), 7)),
        dma((2, len(PARTS), 7)),
        dma((ng - 1,)),
        dma((2, ng - 1)),
        dma((ny - 1,)),
        dma((2, ny - 1)),
        dma((nz - 1,)),
        dma((2, nz - 1)),
        dma((2,)),
        dma((2, 2)),
    ]
    return pl.pallas_call(
        functools.partial(kernel, (nz, nr, ng, chans, width, half)),
        out_shape=jax.ShapeDtypeStruct(wavefunc.shape, F32),
        in_specs=[hbm] * 7,
        out_specs=hbm,
        scratch_shapes=scratch,
        compiler_params=pltpu.CompilerParams(
            collective_id=0, has_side_effects=True, vmem_limit_bytes=48 << 20
        ),
        name="cn_step",
    )(
        *(
            pltpu.with_memory_space_constraint(x, pltpu.HBM)
            for x in (
                wavefunc,
                orbitals,
                channel_orbital.reshape(1, chans),
                channel_l.reshape(1, chans),
                row_order.reshape(1, rows),
                density,
                coupling.T,
            )
        )
    )


def solution(mesh):
    placed = (
        P(None, "chan", "rad"),
        P(None, "rad"),
        P("chan"),
        P("chan"),
        P(),
        P(None, "chan"),
        P("chan", None),
    )
    return jax.shard_map(
        functools.partial(body, mesh.shape["chan"], mesh.shape["rad"]),
        mesh=mesh,
        in_specs=placed,
        out_specs=P(None, "chan", "rad"),
        check_vma=False,
    )
```

```python
import functools

import jax
import jax.numpy as jnp
from jax import lax
from jax.experimental import pallas as pl
from jax.experimental.pallas import tpu as pltpu
from jax.sharding import PartitionSpec as P

SWEEPS = 4
MESH = pl.DeviceIdType.MESH
F32 = jnp.float32
BF16 = jnp.bfloat16
LANES = 128
SPAN = 400.0 / 408.0

RS_PLAN = ((-4, -2), (-3, -1), (3, 1), (-1, -1), (1, 1), (-2, -2), (2, 2))
AG_PLAN = ((0, 2), (0, -2), (0, 1), (0, -1), (-2, 2), (-2, 1), (2, -1))
PARTS = ((0, 40), (40, 32))
WHOLE = (0, 72)
RS_WHOLE = (3, 4)
AG_WHOLE = (2, 3)
ROWS_STEP = 32


def split2(x):
    hi = x.astype(BF16)
    return hi, (x - hi.astype(F32)).astype(BF16)


def dot(a, b):
    return jnp.dot(a, b, preferred_element_type=F32)


def as_column(row):
    eight = jnp.broadcast_to(row, (8, row.shape[1]))
    first = lax.broadcasted_iota(jnp.int32, (8, LANES), 0) == 0
    return lax.dot_general(
        eight,
        jnp.where(first, 1.0, 0.0).astype(F32),
        (((0,), (0,)), ((), ())),
        precision=lax.Precision.HIGHEST,
        preferred_element_type=F32,
    )


def kernel(
    sizes,
    wave_hbm,
    orbitals_hbm,
    which_hbm,
    ell_hbm,
    order_hbm,
    density_hbm,
    coupling_hbm,
    out_hbm,
    orbitals_ref,
    which_ref,
    ell_ref,
    order_ref,
    density_ref,
    coupling_ref,
    vbuf,
    rhs,
    orb,
    diag,
    scl,
    known,
    alpha,
    beta,
    field,
    w_hi,
    w_lo,
    up_t,
    dn_t,
    d_both,
    f_both,
    rho,
    pot,
    rsbuf,
    own,
    tin01,
    sc_in,
    sc_out,
    ca_src,
    ca_buf,
    cb_src,
    cb_buf,
    cc_src,
    cc_buf,
    io_sem,
    rs_s,
    rs_r,
    ag_s,
    ag_r,
    ca_s,
    ca_r,
    cb_s,
    cb_r,
    cc_s,
    cc_r,
    ha_s,
    ha_r,
):
    nz, nr, ng, chans, width, half = sizes
    ny = nr // ng
    z = lax.axis_index("chan")
    r = lax.axis_index("rad")
    g = lax.rem(r, ng)
    y = lax.div(r, ng)
    total_rows = width * nr
    delta = SPAN / total_rows

    def zdev(offset):
        return (lax.rem(z + offset + nz, nz), r)

    sign = 1 - 2 * lax.rem(r, 2)

    def near(offset):
        return lax.rem(z + sign * offset + nz, nz)

    def gdev(k):
        return (z, y * ng + lax.rem(g + k, ng))

    def ydev(k):
        return (z, lax.rem(y + k, ny) * ng + g)

    barrier = pltpu.get_barrier_semaphore()

    def greet(device):
        pl.semaphore_signal(barrier, inc=1, device_id=device, device_id_type=MESH)

    for k in (1, 2, nz - 2, nz - 1):
        greet(zdev(k))
    for k in range(1, ng):
        greet(gdev(k))
    for k in range(1, ny):
        greet(ydev(k))
    greet((z, lax.rem(r + 1, nr)))
    greet((z, lax.rem(r + nr - 1, nr)))

    loads = [
        pltpu.make_async_copy(src, dst, io_sem.at[i])
        for i, (src, dst) in enumerate(
            (
                (which_hbm, which_ref),
                (orbitals_hbm, orbitals_ref),
                (wave_hbm, vbuf.at[0, :, :, pl.ds(LANES, width)]),
                (density_hbm, density_ref),
                (order_hbm, order_ref),
                (ell_hbm, ell_ref),
                (coupling_hbm, coupling_ref),
            )
        )
    ]
    for load in loads:
        load.start()

    @pl.when(r == 0)
    def _():
        for par in range(2):
            for p in range(2):
                vbuf[par, p, :, 0:LANES] = jnp.zeros((chans, LANES), F32)

    @pl.when(r == nr - 1)
    def _():
        for par in range(2):
            for p in range(2):
                vbuf[par, p, :, LANES + width :] = jnp.zeros((chans, LANES), F32)

    tiles = width // LANES
    i0 = lax.broadcasted_iota(jnp.int32, (2 * LANES, 2 * LANES), 0)
    i1 = lax.broadcasted_iota(jnp.int32, (2 * LANES, 2 * LANES), 1)
    inner = (i0 < LANES) & (i1 < LANES) & (i0 <= i1)
    outer = (i0 >= LANES) & (i1 >= LANES) & (i0 > i1)
    tri = jnp.where(inner | outer, 1.0, 0.0).astype(BF16)
    lane4 = lax.broadcasted_iota(jnp.int32, (4, LANES), 1)
    lane_id = lax.broadcasted_iota(jnp.int32, (half, LANES), 1)

    def spread_orbitals():
        which = as_column(which_ref[...].astype(F32))
        for t in range(tiles):
            lanes = slice(t * LANES, (t + 1) * LANES)
            for c0 in range(0, chans, ROWS_STEP):
                rows = slice(c0, c0 + ROWS_STEP)
                pick = which[rows]
                value = jnp.zeros((ROWS_STEP, LANES), F32)
                for o in range(orbitals_ref.shape[0]):
                    value = jnp.where(pick == float(o), orbitals_ref[o : o + 1, lanes], value)
                orb[rows, lanes] = value

    def split_density():
        hi, lo = split2(density_ref[...])
        d_both[: 2 * half] = hi
        d_both[2 * half :] = lo

    def radius_of(t):
        lane = lax.broadcasted_iota(jnp.int32, (1, LANES), 1)
        index = (r * width + t * LANES + lane).astype(F32)
        return 8.0 + 400.0 * (index + 0.5) / total_rows

    def power_tables():
        order = as_column(order_ref[...].astype(F32))
        for t in range(tiles):
            scaled = radius_of(t) / 408.0
            up = jnp.exp(order * jnp.log(scaled))
            dn = 1.0 / (up * scaled)
            inv_dn = jnp.broadcast_to((up * scaled)[:, LANES - 1 :], up.shape)
            inv_up = jnp.broadcast_to((dn * scaled)[:, :1], up.shape)
            for mh in range(2):
                rows = slice(mh * half, (mh + 1) * half)
                up_t[t, mh] = up[rows]
                dn_t[t, mh] = dn[rows]
                sc_in[t, mh] = inv_dn[rows]
                sc_out[t, mh] = inv_up[rows]

    def diagonal_tables():
        ell = as_column(ell_ref[...].astype(F32))
        strength = ell * (ell + 1.0)
        for t in range(tiles):
            radius = radius_of(t)
            inv = 1.0 / (4.0 * radius * radius)
            lanes = slice(t * LANES, (t + 1) * LANES)
            for c0 in range(0, chans, ROWS_STEP):
                rows = slice(c0, c0 + ROWS_STEP)
                dg = 0.5 + strength[rows] * inv
                sc = 1.0 / (1.0 + dg * dg)
                al = sc * orb[rows, lanes]
                diag[rows, lanes] = dg
                scl[rows, lanes] = sc
                alpha[rows, lanes] = al
                beta[rows, lanes] = al * dg
        turned = jnp.concatenate(
            [coupling_ref[...], jnp.zeros((chans - 2 * half, chans), F32)], axis=0
        )
        hi, lo = split2(jnp.transpose(turned)[:, : 2 * half])
        f_both[:chans] = hi
        f_both[chans:] = lo

    def rs_copy(pc, part, i):
        chunk, target = RS_PLAN[i]
        rows = pl.ds(*(WHOLE if i in RS_WHOLE else PARTS[part]))
        return pltpu.make_async_remote_copy(
            src_ref=rho.at[pc, near(chunk), rows],
            dst_ref=rsbuf.at[pc, i, rows],
            send_sem=rs_s.at[pc, part, i],
            recv_sem=rs_r.at[pc, part, i],
            device_id=(near(target), r),
            device_id_type=MESH,
        )

    def ag_copy(pc, part, i):
        chunk, target = AG_PLAN[i]
        rows = pl.ds(*(WHOLE if i in AG_WHOLE else PARTS[part]))
        place = pot.at[pc, near(chunk), rows]
        return pltpu.make_async_remote_copy(
            src_ref=place,
            dst_ref=place,
            send_sem=ag_s.at[pc, part, i],
            recv_sem=ag_r.at[pc, part, i],
            device_id=(near(target), r),
            device_id_type=MESH,
        )

    def small_copy(src, buf, send, recv, par, k, device):
        return pltpu.make_async_remote_copy(
            src_ref=src,
            dst_ref=buf.at[par, k - 1],
            send_sem=send.at[k - 1],
            recv_sem=recv.at[par, k - 1],
            device_id=device,
            device_id_type=MESH,
        )

    def ca_copy(par, k):
        return small_copy(ca_src, ca_buf, ca_s, ca_r, par, k, gdev(k))

    def cb_copy(par, k):
        return small_copy(cb_src, cb_buf, cb_s, cb_r, par, k, ydev(k))

    def cc_copy(par, k):
        return small_copy(cc_src, cc_buf, cc_s, cc_r, par, k, zdev(k))

    def halo_copy(par, side):
        here, there = (width, 0) if side == 0 else (LANES, LANES + width)
        to = r + 1 if side == 0 else r - 1
        to = lax.rem(to + nr, nr)
        return pltpu.make_async_remote_copy(
            src_ref=vbuf.at[par, :, :, pl.ds(here, LANES)],
            dst_ref=vbuf.at[par, :, :, pl.ds(there, LANES)],
            send_sem=ha_s.at[side],
            recv_sem=ha_r.at[par, side],
            device_id=(z, to),
            device_id_type=MESH,
        )

    def weigh(par, pc):
        lanes = slice(pc * 2 * LANES, (pc + 1) * 2 * LANES)
        for c0 in range(0, chans, ROWS_STEP):
            rows = slice(c0, c0 + ROWS_STEP)
            for p in range(2):
                v = vbuf[par, p, rows, LANES + lanes.start : LANES + lanes.stop]
                hi, lo = split2(v * orb[rows, lanes])
                w_hi[p, rows] = hi
                w_lo[p, rows] = lo

    def densities(pc):
        rows = 2 * half
        for p in range(2):
            wide = dot(d_both[...], w_hi[p])
            part = wide[:rows] + (wide[rows:] + dot(d_both[:rows], w_lo[p]))
            for mh in range(2):
                for h in range(2):
                    rho[pc, 4 * p + 2 * mh + h] = part[
                        mh * half : (mh + 1) * half, h * LANES : (h + 1) * LANES
                    ]

    def prepare(n, par, pc):
        base = pc * 2 * LANES
        lanes = slice(base, base + 2 * LANES)

        def kinetic(rows):
            v, kin = [], []
            for p in range(2):
                x = vbuf[par, p, rows, pl.ds(base, 4 * LANES)]
                left = pltpu.roll(x, 1, 1)[:, LANES : 3 * LANES]
                right = pltpu.roll(x, 4 * LANES - 1, 1)[:, LANES : 3 * LANES]
                v.append(x[:, LANES : 3 * LANES])
                kin.append(-0.25 * (left + right))
            return v, kin

        @pl.when(n == 0)
        def _():
            for c0 in range(0, chans, ROWS_STEP):
                rows = slice(c0, c0 + ROWS_STEP)
                v, kin = kinetic(rows)
                dg = diag[rows, lanes]
                rhs[0, rows, lanes] = v[0] + (kin[1] + dg * v[1])
                rhs[1, rows, lanes] = v[1] - (kin[0] + dg * v[0])

        @pl.when(n == 1)
        def _():
            for c0 in range(0, chans, ROWS_STEP):
                rows = slice(c0, c0 + ROWS_STEP)
                ob = orb[rows, lanes]
                rhs[0, rows, lanes] = rhs[0, rows, lanes] + field[pc, 1, rows] * ob
                rhs[1, rows, lanes] = rhs[1, rows, lanes] - field[pc, 0, rows] * ob

        for c0 in range(0, chans, ROWS_STEP):
            rows = slice(c0, c0 + ROWS_STEP)
            v, kin = kinetic(rows)
            dg = diag[rows, lanes]
            sc = scl[rows, lanes]
            q0 = rhs[0, rows, lanes] + kin[1]
            q1 = rhs[1, rows, lanes] - kin[0]
            known[0, rows, lanes] = (q0 + dg * q1) * sc
            known[1, rows, lanes] = (q1 - dg * q0) * sc

    def send_far(pc):
        for part in range(len(PARTS)):
            for i in (0, 2, 1):
                rs_copy(pc, part, i).start()

    def send_direct(pc):
        for i in RS_WHOLE:
            rs_copy(pc, 0, i).start()

    def totals():
        acc = jnp.zeros((half, LANES), F32)
        for p in range(2):
            for mh in range(2):
                blocks = [rho[t // 2, 4 * p + 2 * mh + t % 2] * delta for t in range(tiles)]
                ups = [blocks[t] * up_t[t, mh] for t in range(tiles)]
                dns = [blocks[t] * dn_t[t, mh] for t in range(tiles)]
                near_out = dns[0] + dns[1]
                far_out = dns[2] + dns[3]
                sums = ((ups[0] + ups[1]) + (ups[2] + ups[3]), near_out + far_out, far_out)
                for kind in range(3):
                    s = jnp.sum(sums[kind], axis=1, keepdims=True)
                    acc = jnp.where(lane_id == kind * 4 + p * 2 + mh, s, acc)
        full = jnp.concatenate([acc, jnp.zeros((LANES - half, LANES), F32)], axis=0)
        own[...] = jnp.transpose(full)[0:16]
        ca_src[0] = own[0:4]
        ca_src[1] = own[4:8]

    def send_totals(par):
        for k in range(1, ng):
            ca_copy(par, k).start()

        @pl.when(r < nr - 1)
        def _():
            halo_copy(par, 0).start()

        @pl.when(r > 0)
        def _():
            halo_copy(par, 1).start()

    def communicate(n, par):
        for pc in range(2):
            for part in range(len(PARTS)):
                rows = pl.ds(*PARTS[part])
                rs_copy(pc, part, 0).wait_recv()
                rs_copy(pc, part, 1).wait_recv()
                at = near(-2)
                rho[pc, at, rows] = rho[pc, at, rows] + rsbuf[pc, 0, rows] + rsbuf[pc, 1, rows]
                rs_copy(pc, part, 5).start()
                rs_copy(pc, part, 2).wait_recv()
                at = near(2)
                rho[pc, at, rows] = rho[pc, at, rows] + rsbuf[pc, 2, rows]
                rs_copy(pc, part, 6).start()
            if pc == 0:
                send_direct(1)
        below = jnp.zeros((4, LANES), F32)
        above = jnp.zeros((4, LANES), F32)
        whole_in = ca_src[0]
        whole_out = ca_src[1]
        for k in range(1, ng):
            ca_copy(par, k).wait_recv()
            peer = lax.rem(g - k + ng, ng)
            got_in = ca_buf[par, k - 1, 0]
            got_out = ca_buf[par, k - 1, 1]
            below = below + got_in * jnp.where(peer < g, 1.0, 0.0).astype(F32)
            above = above + got_out * jnp.where(peer > g, 1.0, 0.0).astype(F32)
            whole_in = whole_in + got_in
            whole_out = whole_out + got_out
        cb_src[0] = whole_in
        cb_src[1] = whole_out
        for k in range(1, ny):
            cb_copy(par, k).start()

        quarter = lax.rem(lax.div(z, 2), 2)
        for pc in range(2):
            tile = 2 * pc + lax.rem(z, 2)
            for part in range(len(PARTS)):
                size = PARTS[part][1]
                rows = pl.ds(*PARTS[part])
                for i in (5, 6) if part else (3, 4, 5, 6):
                    rs_copy(pc, part, i).wait_recv()
                acc = (rho[pc, z, rows] + rsbuf[pc, 3, rows]) + (
                    rsbuf[pc, 4, rows] + rsbuf[pc, 5, rows]
                )
                acc = (acc + rsbuf[pc, 6, rows]) * delta
                up = up_t[tile, quarter, rows]
                dn = dn_t[tile, quarter, rows]

                pair = jnp.concatenate([acc * up, acc * dn], axis=1)
                hi = pair.astype(BF16).astype(F32)
                sums = dot(jnp.concatenate([hi, pair - hi], axis=0).astype(BF16), tri)
                sums = sums[:size] + sums[size:]
                pot[pc, z, rows] = dn * sums[:, :LANES] + up * sums[:, LANES:]
                for i in (0, 1):
                    ag_copy(pc, part, i).start()
            if pc == 0:
                for i in AG_WHOLE:
                    ag_copy(pc, 0, i).start()
        for k in range(1, ny):
            cb_copy(par, k).wait_recv()
            peer = lax.rem(y - k + ny, ny)
            below = below + cb_buf[par, k - 1, 0] * jnp.where(peer < y, 1.0, 0.0).astype(F32)
            above = above + cb_buf[par, k - 1, 1] * jnp.where(peer > y, 1.0, 0.0).astype(F32)
        far = own[8:12]
        cc_src[0] = jnp.where(lane4 < half, below, pltpu.roll(far, half, 1))
        cc_src[1] = jnp.where(lane4 < half, above, pltpu.roll(far, 2 * half - LANES, 1))
        for k in range(1, nz):
            cc_copy(par, k).start()

        @pl.when(r < nr - 1)
        def _():
            halo_copy(par, 0).wait_send()
            halo_copy(par, 1).wait_recv()

        @pl.when(r > 0)
        def _():
            halo_copy(par, 1).wait_send()
            halo_copy(par, 0).wait_recv()

        prepare(n, par, 0)
        for pc in range(2):
            for part in range(len(PARTS)):
                ag_copy(pc, part, 0).wait_recv()
                ag_copy(pc, part, 4).start()
                ag_copy(pc, part, 5).start()
                ag_copy(pc, part, 1).wait_recv()
                ag_copy(pc, part, 6).start()
            if pc == 0:
                for i in AG_WHOLE:
                    ag_copy(1, 0, i).start()
        prepare(n, par, 1)
        carry = [cc_src[kind] for kind in range(2)]
        for k in range(1, nz):
            cc_copy(par, k).wait_recv()
            carry = [carry[kind] + cc_buf[par, k - 1, kind] for kind in range(2)]
        for pc in range(2):
            for part in range(len(PARTS)):
                for i in range(7):
                    if part == 0 or i not in RS_WHOLE:
                        rs_copy(pc, part, i).wait_send()
        for k in range(1, ng):
            ca_copy(par, k).wait_send()
        for k in range(1, ny):
            cb_copy(par, k).wait_send()
        for k in range(1, nz):
            cc_copy(par, k).wait_send()

        first = pltpu.roll(carry[0], LANES - half, 1)
        second = pltpu.roll(carry[1], 2 * LANES - 2 * half, 1)
        far = jnp.where(lane4 < LANES - half, first, second)
        own[0:4] = carry[0]
        own[4:8] = carry[1] + far
        own[8:12] = carry[1]
        pad = jnp.zeros((LANES - 16, LANES), F32)
        return jnp.transpose(jnp.concatenate([own[...], pad], axis=0))[:half]

    def advance(n, par, pc, carry):
        base = pc * 2 * LANES
        for part in range(len(PARTS)):
            for i in (4, 5, 6) if part else (2, 3, 4, 5, 6):
                ag_copy(pc, part, i).wait_recv()
        for p in range(2):
            cols = [[], []]
            for mh in range(2):
                k = 2 * p + mh
                t = 2 * pc
                first_pot = pot[pc, 4 * p + 2 * mh]
                second_pot = pot[pc, 4 * p + 2 * mh + 1]
                wide = (half, LANES)
                below = jnp.broadcast_to(carry[:, k : k + 1], wide)
                at = 4 * (pc + 1) + k
                above = jnp.broadcast_to(carry[:, at : at + 1], wide)
                in_first = jnp.broadcast_to(first_pot[:, LANES - 1 :], wide) * sc_in[t, mh]
                out_second = jnp.broadcast_to(second_pot[:, :1], wide) * sc_out[t + 1, mh]
                if pc == 0:
                    in_second = jnp.broadcast_to(second_pot[:, LANES - 1 :], wide)
                    tin01[k] = in_first + in_second * sc_in[t + 1, mh]
                else:
                    below = below + tin01[k]
                cols[0].append(
                    first_pot + dn_t[t, mh] * below + up_t[t, mh] * (above + out_second)
                )
                cols[1].append(
                    second_pot + dn_t[t + 1, mh] * (below + in_first) + up_t[t + 1, mh] * above
                )
            cols = [jnp.concatenate(parts, axis=0) for parts in cols]
            hi, lo = split2(jnp.concatenate(cols, axis=1))
            wide = dot(f_both[...], hi)
            field[pc, p] = wide[:chans] + (wide[chans:] + dot(f_both[:chans], lo))
        factor = jnp.where(n == 0, 2.0, 1.0).astype(F32)
        lanes = slice(base, base + 2 * LANES)
        for c0 in range(0, chans, ROWS_STEP):
            rows = slice(c0, c0 + ROWS_STEP)
            al = alpha[rows, lanes] * factor
            be = beta[rows, lanes] * factor
            ob = orb[rows, lanes]
            f0 = field[pc, 0, rows]
            f1 = field[pc, 1, rows]
            new = (
                known[0, rows, lanes] + (al * f1 - be * f0),
                known[1, rows, lanes] - (al * f0 + be * f1),
            )
            for p in range(2):
                vbuf[1 - par, p, rows, pl.ds(LANES + base, 2 * LANES)] = new[p]
                hi, lo = split2(new[p] * ob)
                w_hi[p, rows] = hi
                w_lo[p, rows] = lo

    loads[0].wait()
    loads[1].wait()
    spread_orbitals()
    loads[2].wait()
    weigh(0, 0)
    loads[3].wait()
    split_density()
    densities(0)
    pl.semaphore_wait(barrier, 4 + (ng - 1) + (ny - 1) + 2)
    send_far(0)
    send_direct(0)
    weigh(0, 1)
    densities(1)
    send_far(1)
    loads[4].wait()
    power_tables()
    totals()
    send_totals(0)
    loads[5].wait()
    loads[6].wait()
    diagonal_tables()

    def store(pc):
        at = pc * 2 * LANES
        return pltpu.make_async_copy(
            vbuf.at[SWEEPS % 2, :, :, pl.ds(LANES + at, 2 * LANES)],
            out_hbm.at[:, :, pl.ds(at, 2 * LANES)],
            io_sem.at[pc],
        )

    def sweep(n, c):
        par = lax.rem(n, 2)
        carry = communicate(n, par)
        for pc in range(2):
            advance(n, par, pc, carry)

            @pl.when(n < SWEEPS - 1)
            def _():
                densities(pc)

            for part in range(len(PARTS)):
                for i in range(7):
                    if part == 0 or i not in AG_WHOLE:
                        ag_copy(pc, part, i).wait_send()

            @pl.when(n < SWEEPS - 1)
            def _():
                send_far(pc)
                if pc == 0:
                    send_direct(0)

            @pl.when(n == SWEEPS - 1)
            def _():
                store(pc).start()

        @pl.when(n < SWEEPS - 1)
        def _():
            totals()
            send_totals(1 - par)

        return c

    lax.fori_loop(0, SWEEPS, sweep, 0)
    for pc in range(2):
        store(pc).wait()


def body(nz, nr, wavefunc, orbitals, channel_orbital, channel_l, row_order, density, coupling):
    chans, width = wavefunc.shape[1:]
    rows = row_order.shape[0]
    half = rows // 2
    ng = 8 if nr % 8 == 0 else 2
    ny = nr // ng
    hbm = pl.BlockSpec(memory_space=pl.ANY)
    dma = pltpu.SemaphoreType.DMA
    scratch = [
        pltpu.VMEM(orbitals.shape, F32),
        pltpu.VMEM((1, chans), jnp.int32),
        pltpu.VMEM((1, chans), jnp.int32),
        pltpu.VMEM((1, rows), jnp.int32),
        pltpu.VMEM((rows, chans), F32),
        pltpu.VMEM((rows, chans), F32),
        pltpu.VMEM((2, 2, chans, width + 2 * LANES), F32),
        pltpu.VMEM((2, chans, width), F32),
        pltpu.VMEM((chans, width), F32),
        pltpu.VMEM((chans, width), F32),
        pltpu.VMEM((chans, width), F32),
        pltpu.VMEM((2, chans, width), F32),
        pltpu.VMEM((chans, width), F32),
        pltpu.VMEM((chans, width), F32),
        pltpu.VMEM((2, 2, chans, 2 * LANES), F32),
        pltpu.VMEM((2, chans, 2 * LANES), BF16),
        pltpu.VMEM((2, chans, 2 * LANES), BF16),
        pltpu.VMEM((4, 2, half, LANES), F32),
        pltpu.VMEM((4, 2, half, LANES), F32),
        pltpu.VMEM((2 * rows, chans), BF16),
        pltpu.VMEM((2 * chans, rows), BF16),
        pltpu.VMEM((2, 8, half, LANES), F32),
        pltpu.VMEM((2, 8, half, LANES), F32),
        pltpu.VMEM((2, 7, half, LANES), F32),
        pltpu.VMEM((16, LANES), F32),
        pltpu.VMEM((4, half, LANES), F32),
        pltpu.VMEM((4, 2, half, LANES), F32),
        pltpu.VMEM((4, 2, half, LANES), F32),
        pltpu.VMEM((2, 4, LANES), F32),
        pltpu.VMEM((2, ng - 1, 2, 4, LANES), F32),
        pltpu.VMEM((2, 4, LANES), F32),
        pltpu.VMEM((2, ny - 1, 2, 4, LANES), F32),
        pltpu.VMEM((2, 4, LANES), F32),
        pltpu.VMEM((2, nz - 1, 2, 4, LANES), F32),
        dma((7,)),
        dma((2, len(PARTS), 7)),
        dma((2, len(PARTS), 7)),
        dma((2, len(PARTS), 7)),
        dma((2, len(PARTS), 7)),
        dma((ng - 1,)),
        dma((2, ng - 1)),
        dma((ny - 1,)),
        dma((2, ny - 1)),
        dma((nz - 1,)),
        dma((2, nz - 1)),
        dma((2,)),
        dma((2, 2)),
    ]
    return pl.pallas_call(
        functools.partial(kernel, (nz, nr, ng, chans, width, half)),
        out_shape=jax.ShapeDtypeStruct(wavefunc.shape, F32),
        in_specs=[hbm] * 7,
        out_specs=hbm,
        scratch_shapes=scratch,
        compiler_params=pltpu.CompilerParams(
            collective_id=0, has_side_effects=True, vmem_limit_bytes=48 << 20
        ),
        name="cn_step",
    )(
        *(
            pltpu.with_memory_space_constraint(x, pltpu.HBM)
            for x in (
                wavefunc,
                orbitals,
                channel_orbital.reshape(1, chans),
                channel_l.reshape(1, chans),
                row_order.reshape(1, rows),
                density,
                coupling.T,
            )
        )
    )


def solution(mesh):
    placed = (
        P(None, "chan", "rad"),
        P(None, "rad"),
        P("chan"),
        P("chan"),
        P(),
        P(None, "chan"),
        P("chan", None),
    )
    return jax.shard_map(
        functools.partial(body, mesh.shape["chan"], mesh.shape["rad"]),
        mesh=mesh,
        in_specs=placed,
        out_specs=P(None, "chan", "rad"),
        check_vma=False,
    )
```
